32 devices in a mesh: grp: 4 (over y, core), tile: 8 (over z, x).
Axes of the slice: x: 2, y: 2, z: 4, core: 2. Of those that a mesh axis runs over, the one named last changes fastest.
Arguments:
- adjoint_state: float32 [64, 128, 2048], P('tile', 'grp'), may hold values from -6 to 6
- misfit: float32 [64, 128, 2048], P('tile', 'grp'), may hold values from -4 to 4
- east_speed: float32 [64, 128, 2048], P('tile', 'grp'), may hold values from -0.6 to 0.6
- north_speed: float32 [64, 128, 2048], P('tile', 'grp'), may hold values from -0.6 to 0.6
- land_mask: int32 [64, 128, 2048], P('tile', 'grp'), may hold values 0 or 1
- warming_forcing_selector: int32 [128, 2048], P('grp', 'tile'), may hold values 0 or 1
- vertical_filter_matrix: float32 [64, 64], replicated, may hold values from 0 to 0.54
Outputs:
- filtered_thermal_sensitivity: float32 [64, 128, 2048], P('tile', 'grp')
- boundary_warming_sensitivity: float32 [128, 2048], P('grp', 'tile')
The draws below stay inside these ranges and needn't reach their ends.
All inputs are finite; a program needn't handle non-finite values. No bound on the sum of `land_mask` or of `warming_forcing_selector` on one device may be relied on, other than what follows from the above.
Results may differ from the reference program's by a relative error of at most 0.000088.
Values sent between devices are 32-bit elements; how exact they have to be, the bound alone decides.
A program may use at most 192 MiB of HBM per device.

```python
import jax
import jax.numpy as jnp
from jax import lax

LEV = 64
STEPS = 2
NY = 128
NX = 2048


def draw_vertical_filter_matrix(key, part):
    depth_level_index = jnp.arange(LEV)
    spacing_between = jnp.abs(depth_level_index[:, None] - depth_level_index[None, :]).astype(jnp.float32)
    factor = jax.random.uniform(key, (LEV, LEV), jnp.float32, 0.5, 1.5)
    return 0.3 * jnp.exp(-spacing_between / 3.0) * factor


def with_ends(result, key, least, high):
    spot = [jax.random.randint(jax.random.fold_in(key, axis), (), 0, length) for axis, length in enumerate(result.shape)]
    widest = result.shape.index(max(result.shape))
    beside = spot[:widest] + [(spot[widest] + 1) % result.shape[widest]] + spot[widest + 1:]
    return result.at[tuple(spot)].set(least).at[tuple(beside)].set(high)


def steps_of(key, shape, shards, least, high):
    level, own = 1.0, jax.random.fold_in(key, 6)
    for dim, parts in shards:
        draws = jnp.exp(jax.random.uniform(jax.random.fold_in(own, dim), (parts,), jnp.float32, least / len(shards), high / len(shards)))
        level = level * jnp.repeat(draws, shape[dim] // parts).reshape([-1 if axis == dim else 1 for axis in range(len(shape))])
    return level


def centred(key, extent, deviation, reach, split=(), held_as=jnp.bfloat16):
    values = deviation * jax.random.normal(key, extent, jnp.float32)
    if split:
        values = values * steps_of(key, extent, split, -0.22, 0.18)
    return jnp.clip(values, -reach, reach).astype(held_as)


def setup_inputs(seed: int = 0) -> dict:
    key_of = jax.random.split(jax.random.key(seed), 8)
    adjoint_state = centred(key_of[0], (LEV, NY, NX), 1.0, 6.0, ((0, 8), (1, 4)), jnp.float32)
    misfit = centred(key_of[1], (LEV, NY, NX), 0.5, 4.0, ((0, 8), (1, 4)), jnp.float32)
    east_speed = jnp.clip(jax.random.uniform(key_of[2], (LEV, NY, NX), jnp.float32, -0.6, 0.6) * steps_of(key_of[2], (LEV, NY, NX), ((0, 8), (1, 4)), -0.4, 0.0), -0.6, 0.6)
    north_speed = jnp.clip(jax.random.uniform(key_of[3], (LEV, NY, NX), jnp.float32, -0.6, 0.6) * steps_of(key_of[3], (LEV, NY, NX), ((0, 8), (1, 4)), -0.4, 0.0), -0.6, 0.6)
    land_mask = with_ends((jax.random.randint(key_of[4], (LEV, NY, NX), 0, 6) < 5).astype(jnp.int32), jax.random.fold_in(key_of[4], 1), 0, 1)
    warming_forcing_selector = with_ends((jax.random.randint(key_of[5], (NY, NX), 0, 3) < 1).astype(jnp.int32), jax.random.fold_in(key_of[5], 1), 0, 1)
    vertical_filter_matrix = draw_vertical_filter_matrix(jax.random.fold_in(key_of[7], 71), 0)
    return {"adjoint_state": adjoint_state, "misfit": misfit, "east_speed": east_speed, "north_speed": north_speed, "land_mask": land_mask, "warming_forcing_selector": warming_forcing_selector, "vertical_filter_matrix": vertical_filter_matrix}


def advance(padded, misfit, east_speed, north_speed, wet_cells):
    center = padded[1:-1, 1:-1, 1:-1]
    east_cell = padded[1:-1, 1:-1, 2:]
    western_neighbour = padded[1:-1, 1:-1, :-2]
    north_cell = padded[1:-1, 2:, 1:-1]
    south_cell = padded[1:-1, :-2, 1:-1]
    upper_cell = padded[:-2, 1:-1, 1:-1]
    lower_cell = padded[2:, 1:-1, 1:-1]
    vertical = upper_cell + lower_cell - 2.0 * center
    lateral = east_cell + western_neighbour + north_cell + south_cell - 4.0 * center
    change = 0.5 * east_speed * (east_cell - western_neighbour) + 0.5 * north_speed * (north_cell - south_cell)
    return wet_cells * (center + misfit + change + 0.1 * lateral + 0.15 * vertical)


def reference(adjoint_state, misfit, east_speed, north_speed, land_mask, warming_forcing_selector, vertical_filter_matrix):
    wet_cells = land_mask.astype(jnp.float32)
    current_tracer_values = adjoint_state
    for step_index in range(STEPS):
        padded = jnp.pad(current_tracer_values, ((1, 1), (1, 1), (1, 1)))
        current_tracer_values = advance(padded, misfit, east_speed, north_speed, wet_cells)
    filtered_thermal_sensitivity = jnp.einsum("cz,zne->cne", vertical_filter_matrix, current_tracer_values, precision=lax.Precision.HIGHEST)
    boundary_warming_sensitivity = warming_forcing_selector.astype(jnp.float32) * filtered_thermal_sensitivity[0]
    return filtered_thermal_sensitivity, boundary_warming_sensitivity
```

```python
import functools

import jax
import jax.numpy as jnp
from jax import lax
from jax.experimental import pallas as pl
from jax.experimental.pallas import tpu as pltpu
from jax.sharding import PartitionSpec as P

MESH = pl.DeviceIdType.MESH
SUB = 8
LANE = 128
WIDTH = 512
SIDE = 256
HIGHEST = lax.Precision.HIGHEST


def kernel(
    tiles,
    grps,
    state_ref,
    misfit_ref,
    east_ref,
    north_ref,
    land_ref,
    select_ref,
    matrix_ref,
    out_ref,
    surface_ref,
    s0,
    s1,
    s2,
    misfit,
    east,
    north,
    land,
    pencil,
    smooth,
    kron,
    matrix,
    select,
    load_sem,
    level_send,
    level_recv,
    row_send,
    row_recv,
    fwd_send,
    fwd_recv,
    ret_send,
    ret_recv,
):
    levels, rows, columns = state_ref.shape
    chunks = rows // SUB
    part = columns // tiles
    half = tiles // 2
    mine = columns // 2
    near = min(2, levels // 2)
    tile = lax.axis_index("tile")
    grp = lax.axis_index("grp")
    side = lax.div(tile, half)
    inner = (pl.ds(SUB, rows), pl.ds(LANE, columns))

    far_at = pl.multiple_of((1 - side) * mine, LANE)
    near_at = pl.multiple_of(side * mine, LANE)
    first_at = pl.multiple_of((1 - side) * (mine - SIDE), LANE)
    then_at = pl.multiple_of(side * (mine + SIDE), LANE)
    first_width, then_width = mine + SIDE, mine - SIDE

    def load(ref, buf, at, width, k):
        span = pl.ds(at, width)
        return pltpu.make_async_copy(ref.at[:, :, span], buf.at[:, :, span], load_sem.at[k])

    tracer = pltpu.make_async_copy(
        state_ref, s0.at[(pl.ds(1, levels),) + inner], load_sem.at[0]
    )
    fields = ((misfit_ref, misfit), (east_ref, east), (north_ref, north), (land_ref, land))
    loads = [tracer] + [
        load(ref, buf, first_at, first_width, 1 + k) for k, (ref, buf) in enumerate(fields)
    ]
    later = [load(ref, buf, then_at, then_width, 5 + k) for k, (ref, buf) in enumerate(fields)]
    small = [
        pltpu.make_async_copy(matrix_ref, matrix, load_sem.at[9]),
        pltpu.make_async_copy(select_ref, select, load_sem.at[10]),
    ]

    barrier = pltpu.get_barrier_semaphore()

    @pl.loop(1, tiles)
    def _(i):
        other = lax.rem(tile + i, tiles)
        pl.semaphore_signal(barrier, inc=1, device_id=(grp, other), device_id_type=MESH)

    @pl.when(grp > 0)
    def _():
        pl.semaphore_signal(barrier, inc=1, device_id=(grp - 1, tile), device_id_type=MESH)

    @pl.when(grp < grps - 1)
    def _():
        pl.semaphore_signal(barrier, inc=1, device_id=(grp + 1, tile), device_id_type=MESH)

    for copy in loads + later + small:
        copy.start()

    for buf in (s0, s1):
        for start in (0, columns + LANE):
            buf[1 : levels + 1, SUB : SUB + rows, start : start + LANE] = jnp.zeros(
                (levels, rows, LANE), jnp.float32
            )

        @pl.when(tile == 0)
        def _():
            buf[0, SUB : SUB + rows, :] = jnp.zeros((rows, columns + 2 * LANE), jnp.float32)

        @pl.when(tile == tiles - 1)
        def _():
            buf[levels + 1, SUB : SUB + rows, :] = jnp.zeros((rows, columns + 2 * LANE), jnp.float32)

        @pl.when(grp == 0)
        def _():
            buf[1 : levels + 1, 0:SUB, :] = jnp.zeros((levels, SUB, columns + 2 * LANE), jnp.float32)

        @pl.when(grp == grps - 1)
        def _():
            buf[1 : levels + 1, SUB + rows :, :] = jnp.zeros(
                (levels, SUB, columns + 2 * LANE), jnp.float32
            )

    beside = (grp > 0).astype(jnp.int32) + (grp < grps - 1).astype(jnp.int32)

    def level_copies(buf, step):
        top, bottom = state_ref.at[0], state_ref.at[levels - 1]
        if step:
            top, bottom = buf.at[(1,) + inner], buf.at[(levels,) + inner]
        return [
            (
                tile > 0,
                tile < tiles - 1,
                pltpu.make_async_remote_copy(
                    top,
                    buf.at[(levels + 1,) + inner],
                    level_send.at[step, 0],
                    level_recv.at[step, 0],
                    (grp, tile - 1),
                    MESH,
                ),
            ),
            (
                tile < tiles - 1,
                tile > 0,
                pltpu.make_async_remote_copy(
                    bottom,
                    buf.at[(0,) + inner],
                    level_send.at[step, 1],
                    level_recv.at[step, 1],
                    (grp, tile + 1),
                    MESH,
                ),
            ),
        ]

    def row_copies(buf, step, slot, first, count):
        span = pl.ds(first + 1, count)
        across = pl.ds(LANE, columns)
        top, bottom = state_ref.at[:, pl.ds(0, 1), :], state_ref.at[:, pl.ds(rows - 1, 1), :]
        if step:
            top = buf.at[span, pl.ds(SUB, 1), across]
            bottom = buf.at[span, pl.ds(SUB + rows - 1, 1), across]
        return [
            (
                grp > 0,
                grp < grps - 1,
                pltpu.make_async_remote_copy(
                    top,
                    buf.at[span, pl.ds(SUB + rows, 1), across],
                    row_send.at[slot, 0],
                    row_recv.at[slot, 0],
                    (grp - 1, tile),
                    MESH,
                ),
            ),
            (
                grp < grps - 1,
                grp > 0,
                pltpu.make_async_remote_copy(
                    bottom,
                    buf.at[span, pl.ds(SUB - 1, 1), across],
                    row_send.at[slot, 1],
                    row_recv.at[slot, 1],
                    (grp + 1, tile),
                    MESH,
                ),
            ),
        ]

    def start(copies):
        for sends, _, copy in copies:
            pl.when(sends)(copy.start)

    def arrive(copies):
        for _, receives, copy in copies:
            pl.when(receives)(copy.wait_recv)

    def leave(copies):
        for sends, _, copy in copies:
            pl.when(sends)(copy.wait_send)

    def advance(src, dst, pad, first, count, row_first, row_count, at, width, edge=0):
        if count <= 0 or row_count <= 0:
            return
        pieces = [(k, min(WIDTH, width - k)) for k in range(0, width, WIDTH)]

        @pl.loop(0, count * row_count)
        def _(i):
            level = first + lax.div(i, row_count)
            row = pl.multiple_of((row_first + lax.rem(i, row_count)) * SUB, SUB)
            rr = pl.ds(row, SUB)
            middle = pl.ds(row + SUB, SUB)
            for k, wide_by in pieces:
                here = pl.ds(pl.multiple_of(at + k, LANE), wide_by)
                mid = pl.ds(pl.multiple_of(at + k + LANE, LANE), wide_by)
                around = wide_by + 2 * LANE
                wide = src[level + 1, middle, pl.ds(pl.multiple_of(at + k, LANE), around)]
                center = wide[:, LANE : LANE + wide_by]
                e = pltpu.roll(wide, around - 1, 1)[:, LANE : LANE + wide_by]
                w = pltpu.roll(wide, 1, 1)[:, LANE : LANE + wide_by]
                index = lax.broadcasted_iota(jnp.int32, (SUB, wide_by), 0)
                n, s = center, center
                if edge <= 0:
                    down = src[level + 1, pl.ds(row + 2 * SUB, SUB), mid]
                    n = jnp.where(index == 0, down, center)
                if edge >= 0:
                    up = src[level + 1, pl.ds(row, SUB), mid]
                    s = jnp.where(index == SUB - 1, up, center)
                n = pltpu.roll(n, SUB - 1, 0)
                s = pltpu.roll(s, 1, 0)
                a = src[level, middle, mid]
                b = src[level + 2, middle, mid]
                flow = east[level, rr, here] * (e - w) + north[level, rr, here] * (n - s)
                value = (
                    (0.3 * center + misfit[level, rr, here])
                    + 0.5 * flow
                    + (0.1 * ((e + w) + (n + s)) + 0.15 * (a + b))
                )
                value = land[level, rr, here].astype(jnp.float32) * value
                if pad:
                    dst[level + 1, middle, mid] = value
                else:
                    dst[level, rr, here] = value

    def forward(first, count, row_first, row_count, far):
        if count <= 0:
            return
        here = lax.rem(tile, half)
        base = (1 - side) * half if far else side * half
        for r in range(row_first, row_first + row_count):
            span = pl.ds(r * SUB, SUB)
            target = pencil.at[pl.ds(tile * levels + first, count), span, :]

            @pl.loop(0 if far else 1, half)
            def _(i):
                other = base + lax.rem(here + i, half)
                cut = pl.ds(pl.multiple_of(other * part, LANE), part)
                pltpu.make_async_remote_copy(
                    s2.at[pl.ds(first, count), span, cut],
                    target,
                    fwd_send,
                    fwd_recv.at[r],
                    (grp, other),
                    MESH,
                ).start()

            if not far:
                own = pl.ds(pl.multiple_of(tile * part, LANE), part)
                pltpu.make_async_copy(
                    s2.at[pl.ds(first, count), span, own], target, fwd_recv.at[r]
                ).start()

    early = levels - 2 * near
    inside = levels - 2
    far_part, near_part = (far_at, mine), (near_at, mine)
    first_part, then_part = (first_at, first_width), (then_at, then_width)
    every = (0, columns)

    for copy in loads:
        copy.wait()
    advance(s0, s1, True, 1, inside, 0, 1, *first_part, edge=-1)
    advance(s0, s1, True, 1, inside, 1, chunks - 2, *first_part)
    advance(s0, s1, True, 1, inside, chunks - 1, 1, *first_part, edge=1)
    advance(s1, s2, False, near, early, 1, chunks - 2, *far_part)

    pl.semaphore_wait(barrier, tiles - 1 + beside)

    level0 = level_copies(s0, 0)
    row0 = row_copies(s0, 0, 0, 0, levels)
    start(row0)
    start(level0)
    forward(near, early, 1, chunks - 2, True)

    for copy in later + small:
        copy.wait()
    advance(s0, s1, True, 1, inside, 1, chunks - 2, *then_part)
    arrive(row0)
    advance(s0, s1, True, 1, inside, 0, 1, *every)
    advance(s0, s1, True, 1, inside, chunks - 1, 1, *every)
    level1 = level_copies(s1, 1)
    row_mid = row_copies(s1, 1, 1, 1, levels - 2) if levels > 2 else []
    row_ends = row_copies(s1, 1, 2, 0, 1) + row_copies(s1, 1, 3, levels - 1, 1)
    start(row_mid)
    advance(s1, s2, False, near, early, 1, chunks - 2, *near_part)
    forward(near, early, 1, chunks - 2, False)

    arrive(level0)
    advance(s0, s1, True, 0, 1, 0, chunks, *every)
    advance(s0, s1, True, levels - 1, 1, 0, chunks, *every)
    start(level1)
    start(row_ends)

    arrive(row_mid)
    for r in (0, chunks - 1):
        advance(s1, s2, False, near, early, r, 1, *every)
    for r in (0, chunks - 1):
        forward(near, early, r, 1, True)
        forward(near, early, r, 1, False)
    advance(s1, s2, False, 1, near - 1, 0, chunks, *every)
    advance(s1, s2, False, levels - near, near - 1, 0, chunks, *every)

    size = tiles * levels * SUB
    repeat = (
        lax.shift_right_logical(lax.broadcasted_iota(jnp.int32, (size, tiles * levels), 0), 3)
        == lax.broadcasted_iota(jnp.int32, (size, tiles * levels), 1)
    ).astype(jnp.float32)
    tall = jnp.dot(repeat, matrix[...], precision=HIGHEST, preferred_element_type=jnp.float32)
    full = lax.dot_general(
        tall,
        repeat,
        (((1,), (1,)), ((), ())),
        precision=HIGHEST,
        preferred_element_type=jnp.float32,
    )
    same = (lax.broadcasted_iota(jnp.int32, (size, size), 0) & (SUB - 1)) == (
        lax.broadcasted_iota(jnp.int32, (size, size), 1) & (SUB - 1)
    )
    kron[...] = jnp.where(same, full, 0.0)

    arrive(level1)
    arrive(row_ends)
    order = list(range(1, chunks - 1)) + [0, chunks - 1]
    for r in order:
        advance(s1, s2, False, 0, 1, r, 1, *every)
        advance(s1, s2, False, levels - 1, 1, r, 1, *every)
        for far in (True, False):
            forward(0, near, r, 1, far)
            forward(levels - near, near, r, 1, far)

    for r in order:
        span = pl.ds(r * SUB, SUB)
        chunk = pencil.at[:, span, :]
        pltpu.make_async_copy(chunk, chunk, fwd_recv.at[r]).wait()
        result = jnp.dot(
            kron[...],
            pencil[:, r * SUB : (r + 1) * SUB, :].reshape(size, part),
            precision=HIGHEST,
            preferred_element_type=jnp.float32,
        )
        smooth[:, r * SUB : (r + 1) * SUB, :] = result.reshape(tiles * levels, SUB, part)
        home = out_ref.at[:, span, pl.ds(pl.multiple_of(tile * part, LANE), part)]

        def give(other):
            pltpu.make_async_remote_copy(
                smooth.at[pl.ds(other * levels, levels), span, :],
                home,
                ret_send,
                ret_recv,
                (grp, other),
                MESH,
            ).start()

        @pl.loop(0, half)
        def _(i):
            give((1 - side) * half + i)

        @pl.loop(1, half)
        def _(i):
            give(side * half + lax.rem(lax.rem(tile, half) + i, half))

        pltpu.make_async_copy(
            smooth.at[pl.ds(tile * levels, levels), span, :], home, ret_recv
        ).start()
        surface_ref[r * SUB : (r + 1) * SUB, :] = (
            select[r * SUB : (r + 1) * SUB, :].astype(jnp.float32) * result[0:SUB]
        )

    for copies in (level0, row0, level1, row_mid, row_ends):
        leave(copies)
    sent = s2.at[:, :, pl.ds(0, (tiles - 1) * part)]
    pltpu.make_async_copy(sent, sent, fwd_send).wait()
    returned = smooth.at[pl.ds(0, (tiles - 1) * levels)]
    pltpu.make_async_copy(returned, returned, ret_send).wait()
    pltpu.make_async_copy(out_ref, out_ref, ret_recv).wait()


def body(tiles, grps, *args):
    levels, rows, columns = args[0].shape
    part = columns // tiles
    total = tiles * levels
    padded = (levels + 2, rows + 2 * SUB, columns + 2 * LANE)
    block = (levels, rows, columns)
    hbm = pl.BlockSpec(memory_space=pltpu.HBM)
    vmem = pl.BlockSpec(memory_space=pltpu.VMEM)
    return pl.pallas_call(
        functools.partial(kernel, tiles, grps),
        out_shape=(
            pltpu.VMEM(block, jnp.float32),
            pltpu.VMEM((rows, part), jnp.float32),
        ),
        in_specs=[hbm] * 7,
        out_specs=(vmem, vmem),
        scratch_shapes=[
            pltpu.VMEM(padded, jnp.float32),
            pltpu.VMEM(padded, jnp.float32),
            pltpu.VMEM(block, jnp.float32),
            pltpu.VMEM(block, jnp.float32),
            pltpu.VMEM(block, jnp.float32),
            pltpu.VMEM(block, jnp.float32),
            pltpu.VMEM(block, jnp.int32),
            pltpu.VMEM((total, rows, part), jnp.float32),
            pltpu.VMEM((total, rows, part), jnp.float32),
            pltpu.VMEM((total * SUB, total * SUB), jnp.float32),
            pltpu.VMEM((total, total), jnp.float32),
            pltpu.VMEM((rows, part), jnp.int32),
            pltpu.SemaphoreType.DMA((11,)),
            pltpu.SemaphoreType.DMA((2, 2)),
            pltpu.SemaphoreType.DMA((2, 2)),
            pltpu.SemaphoreType.DMA((4, 2)),
            pltpu.SemaphoreType.DMA((4, 2)),
            pltpu.SemaphoreType.DMA,
            pltpu.SemaphoreType.DMA((rows // SUB,)),
            pltpu.SemaphoreType.DMA,
            pltpu.SemaphoreType.DMA,
        ],
        compiler_params=pltpu.CompilerParams(
            collective_id=0, has_side_effects=True, vmem_limit_bytes=40 * 1024 * 1024
        ),
    )(*[pltpu.with_memory_space_constraint(arg, pltpu.HBM) for arg in args])


def solution(mesh):
    split = P("tile", "grp", None)
    return jax.shard_map(
        functools.partial(body, mesh.shape["tile"], mesh.shape["grp"]),
        mesh=mesh,
        in_specs=(split,) * 5 + (P("grp", "tile"), P()),
        out_specs=(split, P("grp", "tile")),
        check_vma=False,
    )
```

```python
import functools

import jax
import jax.numpy as jnp
from jax import lax
from jax.experimental import pallas as pl
from jax.experimental.pallas import tpu as pltpu
from jax.sharding import PartitionSpec as P

MESH = pl.DeviceIdType.MESH
SUB = 8
LANE = 128
WIDTH = 512
HIGHEST = lax.Precision.HIGHEST


def kernel(
    tiles,
    grps,
    state_ref,
    misfit_ref,
    east_ref,
    north_ref,
    land_ref,
    select_ref,
    matrix_ref,
    out_ref,
    surface_ref,
    s0,
    s1,
    s2,
    misfit,
    east,
    north,
    land,
    pencil,
    smooth,
    kron,
    matrix,
    select,
    pencil_u,
    smooth_u,
    border,
    load_sem,
    level_send,
    level_recv,
    row_send,
    row_recv,
    fwd_send,
    fwd_recv,
    ret_send,
    ret_recv,
    border_sem,
):
    levels, rows, columns = state_ref.shape
    chunks = rows // SUB
    part = columns // tiles
    half = tiles // 2
    mine = columns // 2
    near = min(2, levels // 2)
    tile = lax.axis_index("tile")
    grp = lax.axis_index("grp")
    side = lax.div(tile, half)
    uneven = 0
    widths = (part + LANE, part - LANE)
    wide_here = lax.rem(tile, 2) == side
    partner = tile + 1 - 2 * lax.rem(tile, 2)

    def uneven_start(other):
        odd = lax.rem(other, 2)
        shift = odd * (1 - 2 * lax.div(other, half)) * LANE
        return pl.multiple_of(other * part + shift, LANE)

    def by_width(other, run):
        wide = lax.rem(other, 2) == lax.div(other, half)
        pl.when(wide)(lambda: run(widths[0]))
        pl.when(jnp.logical_not(wide))(lambda: run(widths[1]))
    inner = (pl.ds(SUB, rows), pl.ds(LANE, columns))

    early = levels - 2 * near
    inside = levels - 2
    pair = 2 * part
    pairs = half // 2
    parity = lax.rem(tile, 2)
    light = parity == side
    turn = lax.div(lax.rem(tile, half), 2)

    head = side * (pairs - 1)
    lead = (pl.multiple_of(mine - side * pair, LANE), pair)
    rest = (pl.multiple_of((1 - side) * (mine + pair), LANE), mine - pair)
    home = (pl.multiple_of(side * mine, LANE), mine)
    lead_wide = (pl.multiple_of(mine - side * pair - LANE, LANE), pair + 2 * LANE)
    rest_wide = (pl.multiple_of((1 - side) * (mine + pair + LANE), LANE), mine - pair - LANE)
    home_wide = (pl.multiple_of(side * (mine + LANE), LANE), mine - LANE)
    every = (0, columns)

    def load(ref, buf, at, width, k):
        span = pl.ds(at, width)
        return pltpu.make_async_copy(ref.at[:, :, span], buf.at[:, :, span], load_sem.at[k])

    tracer = pltpu.make_async_copy(
        state_ref, s0.at[(pl.ds(1, levels),) + inner], load_sem.at[0]
    )
    fields = ((misfit_ref, misfit), (east_ref, east), (north_ref, north), (land_ref, land))
    loads = [
        [load(ref, buf, *at, 1 + 4 * n + k) for k, (ref, buf) in enumerate(fields)]
        for n, at in enumerate((lead_wide, rest_wide, home_wide))
    ]
    loads[0].insert(0, tracer)
    loads[2] += [
        pltpu.make_async_copy(matrix_ref, matrix, load_sem.at[13]),
        pltpu.make_async_copy(select_ref, select, load_sem.at[14]),
    ]

    barrier = pltpu.get_barrier_semaphore()

    @pl.loop(1, tiles)
    def _(i):
        other = lax.rem(tile + i, tiles)
        pl.semaphore_signal(barrier, inc=1, device_id=(grp, other), device_id_type=MESH)

    @pl.when(grp > 0)
    def _():
        pl.semaphore_signal(barrier, inc=1, device_id=(grp - 1, tile), device_id_type=MESH)

    @pl.when(grp < grps - 1)
    def _():
        pl.semaphore_signal(barrier, inc=1, device_id=(grp + 1, tile), device_id_type=MESH)

    for copy in loads[0] + loads[1] + loads[2]:
        copy.start()

    for buf in (s0, s1):
        for start in (0, columns + LANE):
            buf[1 : levels + 1, SUB : SUB + rows, start : start + LANE] = jnp.zeros(
                (levels, rows, LANE), jnp.float32
            )

        @pl.when(tile == 0)
        def _():
            buf[0, SUB : SUB + rows, :] = jnp.zeros((rows, columns + 2 * LANE), jnp.float32)

        @pl.when(tile == tiles - 1)
        def _():
            buf[levels + 1, SUB : SUB + rows, :] = jnp.zeros((rows, columns + 2 * LANE), jnp.float32)

        @pl.when(grp == 0)
        def _():
            buf[1 : levels + 1, 0:SUB, :] = jnp.zeros((levels, SUB, columns + 2 * LANE), jnp.float32)

        @pl.when(grp == grps - 1)
        def _():
            buf[1 : levels + 1, SUB + rows :, :] = jnp.zeros(
                (levels, SUB, columns + 2 * LANE), jnp.float32
            )

    beside = (grp > 0).astype(jnp.int32) + (grp < grps - 1).astype(jnp.int32)

    def level_copies(buf, step):
        top, bottom = state_ref.at[0], state_ref.at[levels - 1]
        if step:
            top, bottom = buf.at[(1,) + inner], buf.at[(levels,) + inner]
        return [
            (
                tile > 0,
                tile < tiles - 1,
                pltpu.make_async_remote_copy(
                    top,
                    buf.at[(levels + 1,) + inner],
                    level_send.at[step, 0],
                    level_recv.at[step, 0],
                    (grp, tile - 1),
                    MESH,
                ),
            ),
            (
                tile < tiles - 1,
                tile > 0,
                pltpu.make_async_remote_copy(
                    bottom,
                    buf.at[(0,) + inner],
                    level_send.at[step, 1],
                    level_recv.at[step, 1],
                    (grp, tile + 1),
                    MESH,
                ),
            ),
        ]

    def row_copies(buf, step, slot, first, count):
        span = pl.ds(first + 1, count)
        across = pl.ds(LANE, columns)
        top, bottom = state_ref.at[:, pl.ds(0, 1), :], state_ref.at[:, pl.ds(rows - 1, 1), :]
        if step:
            top = buf.at[span, pl.ds(SUB, 1), across]
            bottom = buf.at[span, pl.ds(SUB + rows - 1, 1), across]
        return [
            (
                grp > 0,
                grp < grps - 1,
                pltpu.make_async_remote_copy(
                    top,
                    buf.at[span, pl.ds(SUB + rows, 1), across],
                    row_send.at[slot, 0],
                    row_recv.at[slot, 0],
                    (grp - 1, tile),
                    MESH,
                ),
            ),
            (
                grp < grps - 1,
                grp > 0,
                pltpu.make_async_remote_copy(
                    bottom,
                    buf.at[span, pl.ds(SUB - 1, 1), across],
                    row_send.at[slot, 1],
                    row_recv.at[slot, 1],
                    (grp + 1, tile),
                    MESH,
                ),
            ),
        ]

    def start(copies):
        for sends, _, copy in copies:
            pl.when(sends)(copy.start)

    def arrive(copies):
        for _, receives, copy in copies:
            pl.when(receives)(copy.wait_recv)

    def leave(copies):
        for sends, _, copy in copies:
            pl.when(sends)(copy.wait_send)

    def advance(src, dst, pad, first, count, row_first, row_count, at, width, edge=0, slot=0):
        if count <= 0 or row_count <= 0:
            return
        pieces = [(k, min(WIDTH, width - k)) for k in range(0, width, WIDTH)]

        @pl.loop(0, count * row_count)
        def _(i):
            level = first + lax.div(i, row_count)
            row = pl.multiple_of((row_first + lax.rem(i, row_count)) * SUB, SUB)
            rr = pl.ds(row, SUB)
            middle = pl.ds(row + SUB, SUB)
            for k, wide_by in pieces:
                here = pl.ds(pl.multiple_of(at + k, LANE), wide_by)
                mid = pl.ds(pl.multiple_of(at + k + LANE, LANE), wide_by)
                around = wide_by + 2 * LANE
                wide = src[level + 1, middle, pl.ds(pl.multiple_of(at + k, LANE), around)]
                center = wide[:, LANE : LANE + wide_by]
                e = pltpu.roll(wide, around - 1, 1)[:, LANE : LANE + wide_by]
                w = pltpu.roll(wide, 1, 1)[:, LANE : LANE + wide_by]
                index = lax.broadcasted_iota(jnp.int32, (SUB, wide_by), 0)
                n, s = center, center
                if edge <= 0:
                    down = src[level + 1, pl.ds(row + 2 * SUB, SUB), mid]
                    n = jnp.where(index == 0, down, center)
                if edge >= 0:
                    up = src[level + 1, pl.ds(row, SUB), mid]
                    s = jnp.where(index == SUB - 1, up, center)
                n = pltpu.roll(n, SUB - 1, 0)
                s = pltpu.roll(s, 1, 0)
                a = src[level, middle, mid]
                b = src[level + 2, middle, mid]
                flow = east[level, rr, here] * (e - w) + north[level, rr, here] * (n - s)
                value = (
                    (0.3 * center + misfit[level, rr, here])
                    + 0.5 * flow
                    + (0.1 * ((e + w) + (n + s)) + 0.15 * (a + b))
                )
                value = land[level, rr, here].astype(jnp.float32) * value
                if pad:
                    dst[level + 1, middle, mid] = value
                else:
                    dst[level - first + slot, rr, here] = value

    def forward(first, count, chunk_list, far, same, since, begin=0, end=pairs):
        if count <= 0:
            return
        base = (1 - side if far else side) * half
        base = base + (parity if same else 1 - parity)
        mine_at = pl.ds(tile * levels + first, count)

        def send(r, other, start, width):
            source = s2.at[pl.ds(first, count), pl.ds(r * SUB, SUB), pl.ds(start, width)]
            target = pencil.at[mine_at, pl.ds(r * SUB, SUB), :]
            if r == uneven:
                target = pencil_u.at[mine_at, :, pl.ds(0, width)]
            if other is None:
                pltpu.make_async_copy(source, target, fwd_recv.at[r]).start()
            else:
                pltpu.make_async_remote_copy(
                    source, target, fwd_send, fwd_recv.at[r], (grp, other), MESH
                ).start()

        local = not far and same
        for r in chunk_list:

            @pl.loop(max(begin, 1) if local else begin, end)
            def _(i):
                other = base + 2 * lax.rem(since + i, pairs)
                if r == uneven:
                    by_width(other, lambda width: send(r, other, uneven_start(other), width))
                else:
                    send(r, other, pl.multiple_of(other * part, LANE), part)

            if local:
                if r == uneven:
                    by_width(tile, lambda width: send(r, None, uneven_start(tile), width))
                else:
                    send(r, None, pl.multiple_of(tile * part, LANE), part)

    inner_chunks = list(range(1, chunks - 1))
    outer_chunks = [0, chunks - 1]
    all_chunks = inner_chunks + outer_chunks
    level0 = level_copies(s0, 0)
    row0 = row_copies(s0, 0, 0, 0, levels)

    def enter():
        pl.semaphore_wait(barrier, tiles - 1 + beside)
        start(level0)
        start(row0)

    def first_step(at, width):
        advance(s0, s1, True, 1, inside, 0, 1, at, width, edge=-1)
        advance(s0, s1, True, 1, inside, 1, chunks - 2, at, width)
        advance(s0, s1, True, 1, inside, chunks - 1, 1, at, width, edge=1)

    for copy in loads[0]:
        copy.wait()
    first_step(*lead_wide)
    advance(s1, s2, False, near, early, 1, chunks - 2, *lead)
    enter()
    forward(0, early, inner_chunks, True, True, head, 0, 1)

    for copy in loads[1]:
        copy.wait()
    first_step(*rest_wide)
    advance(s1, s2, False, near, early, 1, chunks - 2, *rest)
    forward(0, early, inner_chunks, True, True, head, 1, pairs)

    for copy in loads[2]:
        copy.wait()
    advance(s0, s1, True, 1, inside, 1, chunks - 2, *home_wide)
    arrive(row0)
    advance(s0, s1, True, 1, inside, 0, 1, *every)
    advance(s0, s1, True, 1, inside, chunks - 1, 1, *every)
    level1 = level_copies(s1, 1)
    row_mid = row_copies(s1, 1, 1, 1, levels - 2) if levels > 2 else []
    row_ends = row_copies(s1, 1, 2, 0, 1) + row_copies(s1, 1, 3, levels - 1, 1)
    start(row_mid)
    advance(s1, s2, False, near, early, 1, chunks - 2, *home)
    arrive(row_mid)
    for r in outer_chunks:
        advance(s1, s2, False, near, early, r, 1, *every)

    @pl.when(light)
    def _():
        forward(0, early, outer_chunks, True, True, turn)

    arrive(level0)
    advance(s0, s1, True, 0, 1, 0, chunks, *every)
    advance(s0, s1, True, levels - 1, 1, 0, chunks, *every)
    start(level1)
    start(row_ends)
    forward(0, early, inner_chunks, True, False, turn)

    @pl.when(light)
    def _():
        forward(0, early, outer_chunks, True, False, turn)


    advance(s1, s2, False, 1, near - 1, 0, chunks, *every, slot=early)
    advance(s1, s2, False, levels - near, near - 1, 0, chunks, *every, slot=early + near - 1)
    forward(early, 2 * near - 2, inner_chunks, True, True, turn)
    forward(early, 2 * near - 2, inner_chunks, True, False, turn)

    @pl.when(light)
    def _():
        forward(early, 2 * near - 2, outer_chunks, True, True, turn)
        forward(early, 2 * near - 2, outer_chunks, True, False, turn)

    forward(0, early, all_chunks, False, True, turn)
    forward(early, 2 * near - 2, all_chunks, False, True, turn)

    total = tiles * levels
    size = total * SUB
    row_of = lax.shift_right_logical(lax.broadcasted_iota(jnp.int32, (size, total), 0), 3)
    level_of = lax.broadcasted_iota(jnp.int32, (size, total), 1)
    repeat = (row_of == level_of).astype(jnp.float32)
    in_tile = lax.rem(row_of, levels)
    natural = jnp.where(
        in_tile < early,
        in_tile + near,
        jnp.where(
            in_tile < levels - 2,
            1 + (in_tile - early) * (levels - 3),
            (in_tile - (levels - 2)) * (levels - 1),
        ),
    )
    pick = (row_of - in_tile + natural == level_of).astype(jnp.float32)
    tall = jnp.dot(repeat, matrix[...], precision=HIGHEST, preferred_element_type=jnp.float32)
    full = lax.dot_general(
        tall,
        pick,
        (((1,), (1,)), ((), ())),
        precision=HIGHEST,
        preferred_element_type=jnp.float32,
    )
    same_row = (lax.broadcasted_iota(jnp.int32, (size, size), 0) & (SUB - 1)) == (
        lax.broadcasted_iota(jnp.int32, (size, size), 1) & (SUB - 1)
    )
    kron[...] = jnp.where(same_row, full, 0.0)

    arrive(level1)
    arrive(row_ends)
    for r in all_chunks:
        advance(s1, s2, False, 0, 1, r, 1, *every, slot=levels - 2)
        advance(s1, s2, False, levels - 1, 1, r, 1, *every, slot=levels - 1)
        for same in (True, False):
            if r in inner_chunks:
                forward(levels - 2, 2, [r], True, same, turn)
            else:
                pl.when(light)(lambda: forward(levels - 2, 2, [r], True, same, turn))
                pl.when(jnp.logical_not(light))(lambda: forward(0, levels, [r], True, same, turn))
        forward(levels - 2, 2, [r], False, True, turn)
        forward(0, levels, [r], False, False, turn)

    def give(source, place):
        def to(other):
            pltpu.make_async_remote_copy(
                source(other), place, ret_send, ret_recv, (grp, other), MESH
            ).start()

        @pl.loop(0, half)
        def _(i):
            to((1 - side) * half + i)

        @pl.loop(1, half)
        def _(i):
            to(side * half + lax.rem(lax.rem(tile, half) + i, half))

        pltpu.make_async_copy(source(tile), place, ret_recv).start()

    def smoothed(block, width):
        return jnp.dot(
            kron[...],
            block.reshape(size, width),
            precision=HIGHEST,
            preferred_element_type=jnp.float32,
        )

    def finish(r):
        span = pl.ds(r * SUB, SUB)
        chunk = pencil.at[:, span, :]
        pltpu.make_async_copy(chunk, chunk, fwd_recv.at[r]).wait()
        result = smoothed(pencil[:, r * SUB : (r + 1) * SUB, :], part)
        smooth[:, r * SUB : (r + 1) * SUB, :] = result.reshape(tiles * levels, SUB, part)
        give(
            lambda other: smooth.at[pl.ds(other * levels, levels), span, :],
            out_ref.at[:, span, pl.ds(pl.multiple_of(tile * part, LANE), part)],
        )
        surface_ref[r * SUB : (r + 1) * SUB, :] = (
            select[r * SUB : (r + 1) * SUB, :].astype(jnp.float32) * result[0:SUB]
        )

    strip = pltpu.make_async_remote_copy(
        smooth_u.at[0, :, pl.ds(pl.multiple_of((1 - side) * part, LANE), LANE)],
        border,
        border_sem.at[0],
        border_sem.at[1],
        (grp, partner),
        MESH,
    )

    def finish_uneven(width):
        span = pl.ds(uneven * SUB, SUB)
        across = pl.ds(0, width)
        chunk = pencil_u.at[:, :, across]
        pltpu.make_async_copy(chunk, chunk, fwd_recv.at[uneven]).wait()
        result = smoothed(pencil_u[:, :, 0:width], width)
        smooth_u[:, :, 0:width] = result.reshape(tiles * levels, SUB, width)
        give(
            lambda other: smooth_u.at[pl.ds(other * levels, levels), :, across],
            out_ref.at[:, span, pl.ds(uneven_start(tile), width)],
        )
        if width > part:
            strip.start()
            own = smooth_u[0, :, pl.ds(pl.multiple_of(side * LANE, LANE), part)]
            surface_ref[span, :] = select[span, :].astype(jnp.float32) * own
        else:
            at = pl.ds(pl.multiple_of((1 - side) * LANE, LANE), width)
            surface_ref[span, at] = select[span, at].astype(jnp.float32) * smooth_u[0, :, across]

    for r in all_chunks:
        if r == uneven:
            by_width(tile, finish_uneven)
        else:
            finish(r)

    def settle(width):
        span = pl.ds(uneven * SUB, SUB)
        if width > part:
            strip.wait_send()
        else:
            strip.wait_recv()
            at = pl.ds(pl.multiple_of(side * width, LANE), LANE)
            surface_ref[span, at] = select[span, at].astype(jnp.float32) * border[...]
        sent = s2.at[:, span, pl.ds(0, columns - width)]
        pltpu.make_async_copy(sent, sent, fwd_send).wait()
        returned = smooth_u.at[pl.ds(0, (tiles - 1) * levels), :, pl.ds(0, width)]
        pltpu.make_async_copy(returned, returned, ret_send).wait()

    by_width(tile, settle)
    for copies in (level0, row0, level1, row_mid, row_ends):
        leave(copies)
    even_rows = pl.ds(0, rows - SUB)
    sent = s2.at[:, even_rows, pl.ds(0, (tiles - 1) * part)]
    pltpu.make_async_copy(sent, sent, fwd_send).wait()
    returned = smooth.at[pl.ds(0, (tiles - 1) * levels), even_rows]
    pltpu.make_async_copy(returned, returned, ret_send).wait()
    pltpu.make_async_copy(out_ref, out_ref, ret_recv).wait()


def body(tiles, grps, *args):
    levels, rows, columns = args[0].shape
    part = columns // tiles
    total = tiles * levels
    padded = (levels + 2, rows + 2 * SUB, columns + 2 * LANE)
    block = (levels, rows, columns)
    hbm = pl.BlockSpec(memory_space=pltpu.HBM)
    vmem = pl.BlockSpec(memory_space=pltpu.VMEM)
    return pl.pallas_call(
        functools.partial(kernel, tiles, grps),
        out_shape=(
            pltpu.VMEM(block, jnp.float32),
            pltpu.VMEM((rows, part), jnp.float32),
        ),
        in_specs=[hbm] * 7,
        out_specs=(vmem, vmem),
        scratch_shapes=[
            pltpu.VMEM(padded, jnp.float32),
            pltpu.VMEM(padded, jnp.float32),
            pltpu.VMEM(block, jnp.float32),
            pltpu.VMEM(block, jnp.float32),
            pltpu.VMEM(block, jnp.float32),
            pltpu.VMEM(block, jnp.float32),
            pltpu.VMEM(block, jnp.int32),
            pltpu.VMEM((total, rows, part), jnp.float32),
            pltpu.VMEM((total, rows, part), jnp.float32),
            pltpu.VMEM((total * SUB, total * SUB), jnp.float32),
            pltpu.VMEM((total, total), jnp.float32),
            pltpu.VMEM((rows, part), jnp.int32),
            pltpu.VMEM((total, SUB, part + LANE), jnp.float32),
            pltpu.VMEM((total, SUB, part + LANE), jnp.float32),
            pltpu.VMEM((SUB, LANE), jnp.float32),
            pltpu.SemaphoreType.DMA((15,)),
            pltpu.SemaphoreType.DMA((2, 2)),
            pltpu.SemaphoreType.DMA((2, 2)),
            pltpu.SemaphoreType.DMA((4, 2)),
            pltpu.SemaphoreType.DMA((4, 2)),
            pltpu.SemaphoreType.DMA,
            pltpu.SemaphoreType.DMA((rows // SUB,)),
            pltpu.SemaphoreType.DMA,
            pltpu.SemaphoreType.DMA,
            pltpu.SemaphoreType.DMA((2,)),
        ],
        compiler_params=pltpu.CompilerParams(
            collective_id=0, has_side_effects=True, vmem_limit_bytes=40 * 1024 * 1024
        ),
    )(*[pltpu.with_memory_space_constraint(arg, pltpu.HBM) for arg in args])


def solution(mesh):
    split = P("tile", "grp", None)
    return jax.shard_map(
        functools.partial(body, mesh.shape["tile"], mesh.shape["grp"]),
        mesh=mesh,
        in_specs=(split,) * 5 + (P("grp", "tile"), P()),
        out_specs=(split, P("grp", "tile")),
        check_vma=False,
    )
```

```python
import functools

import jax
import jax.numpy as jnp
from jax import lax
from jax.experimental import pallas as pl
from jax.experimental.pallas import tpu as pltpu
from jax.sharding import PartitionSpec as P

MESH = pl.DeviceIdType.MESH
SUB = 8
LANE = 128
WIDTH = 512
HIGHEST = lax.Precision.HIGHEST


def kernel(
    tiles,
    grps,
    state_ref,
    misfit_ref,
    east_ref,
    north_ref,
    land_ref,
    select_ref,
    matrix_ref,
    out_ref,
    surface_ref,
    s0,
    s1,
    s2,
    misfit,
    east,
    north,
    land,
    pencil,
    smooth,
    kron,
    matrix,
    select,
    pencil_u,
    smooth_u,
    border,
    load_sem,
    level_send,
    level_recv,
    row_send,
    row_recv,
    fwd_send,
    fwd_recv,
    ret_send,
    ret_recv,
    border_sem,
):
    levels, rows, columns = state_ref.shape
    chunks = rows // SUB
    part = columns // tiles
    half = tiles // 2
    mine = columns // 2
    near = min(2, levels // 2)
    tile = lax.axis_index("tile")
    grp = lax.axis_index("grp")
    side = lax.div(tile, half)
    uneven = 0
    widths = (part + LANE, part - LANE)
    wide_here = lax.rem(tile, 2) == side
    partner = tile + 1 - 2 * lax.rem(tile, 2)

    def uneven_start(other):
        odd = lax.rem(other, 2)
        shift = odd * (1 - 2 * lax.div(other, half)) * LANE
        return pl.multiple_of(other * part + shift, LANE)

    def by_width(other, run):
        wide = lax.rem(other, 2) == lax.div(other, half)
        pl.when(wide)(lambda: run(widths[0]))
        pl.when(jnp.logical_not(wide))(lambda: run(widths[1]))
    inner = (pl.ds(SUB, rows), pl.ds(LANE, columns))

    early = levels - 2 * near
    inside = levels - 2
    pair = 2 * part
    pairs = half // 2
    parity = lax.rem(tile, 2)
    light = parity == side
    turn = lax.div(lax.rem(tile, half), 2)

    head = side * (pairs - 1)
    lead = (pl.multiple_of(mine - side * pair, LANE), pair)
    rest = (pl.multiple_of((1 - side) * (mine + pair), LANE), mine - pair)
    home = (pl.multiple_of(side * mine, LANE), mine)
    lead_wide = (pl.multiple_of(mine - side * pair - LANE, LANE), pair + 2 * LANE)
    rest_wide = (pl.multiple_of((1 - side) * (mine + pair + LANE), LANE), mine - pair - LANE)
    home_wide = (pl.multiple_of(side * (mine + LANE), LANE), mine - LANE)
    every = (0, columns)

    def state_load(at, width, k):
        return pltpu.make_async_copy(
            state_ref.at[:, :, pl.ds(at, width)],
            s0.at[pl.ds(1, levels), pl.ds(SUB, rows), pl.ds(at + LANE, width)],
            load_sem.at[k],
        )

    def field_loads(at, first, count, k):
        span = (pl.ds(first, count), slice(None), pl.ds(*at))
        return [
            pltpu.make_async_copy(ref.at[span], buf.at[span], load_sem.at[k + n])
            for n, (ref, buf) in enumerate(fields)
        ]

    fields = ((misfit_ref, misfit), (east_ref, east), (north_ref, north), (land_ref, land))
    loads = [
        [state_load(pl.multiple_of(mine - side * pair - 2 * LANE, LANE), pair + 4 * LANE, 0)],
        [
            state_load(pl.multiple_of(side * (mine + 2 * LANE), LANE), mine - 2 * LANE, 1),
            state_load(
                pl.multiple_of((1 - side) * (mine + pair + 2 * LANE), LANE),
                mine - pair - 2 * LANE,
                2,
            ),
        ]
        + field_loads(rest_wide, 0, levels, 3),
        field_loads(home_wide, 0, levels, 7)
        + field_loads(lead_wide, 0, 1, 11)
        + field_loads(lead_wide, levels - 1, 1, 15),
    ]
    if inside > 0:
        loads[0] += field_loads(lead_wide, 1, inside, 19)
    loads[2] += [
        pltpu.make_async_copy(matrix_ref, matrix, load_sem.at[23]),
        pltpu.make_async_copy(select_ref, select, load_sem.at[24]),
    ]

    barrier = pltpu.get_barrier_semaphore()

    @pl.loop(1, tiles)
    def _(i):
        other = lax.rem(tile + i, tiles)
        pl.semaphore_signal(barrier, inc=1, device_id=(grp, other), device_id_type=MESH)

    @pl.when(grp > 0)
    def _():
        pl.semaphore_signal(barrier, inc=1, device_id=(grp - 1, tile), device_id_type=MESH)

    @pl.when(grp < grps - 1)
    def _():
        pl.semaphore_signal(barrier, inc=1, device_id=(grp + 1, tile), device_id_type=MESH)

    for copy in loads[0] + loads[1] + loads[2]:
        copy.start()

    for buf in (s0, s1):
        for start in (0, columns + LANE):
            buf[1 : levels + 1, SUB : SUB + rows, start : start + LANE] = jnp.zeros(
                (levels, rows, LANE), jnp.float32
            )

        @pl.when(tile == 0)
        def _():
            buf[0, SUB : SUB + rows, :] = jnp.zeros((rows, columns + 2 * LANE), jnp.float32)

        @pl.when(tile == tiles - 1)
        def _():
            buf[levels + 1, SUB : SUB + rows, :] = jnp.zeros((rows, columns + 2 * LANE), jnp.float32)

        @pl.when(grp == 0)
        def _():
            buf[1 : levels + 1, 0:SUB, :] = jnp.zeros((levels, SUB, columns + 2 * LANE), jnp.float32)

        @pl.when(grp == grps - 1)
        def _():
            buf[1 : levels + 1, SUB + rows :, :] = jnp.zeros(
                (levels, SUB, columns + 2 * LANE), jnp.float32
            )

    beside = (grp > 0).astype(jnp.int32) + (grp < grps - 1).astype(jnp.int32)

    def level_copies(buf, step):
        top, bottom = state_ref.at[0], state_ref.at[levels - 1]
        if step:
            top, bottom = buf.at[(1,) + inner], buf.at[(levels,) + inner]
        return [
            (
                tile > 0,
                tile < tiles - 1,
                pltpu.make_async_remote_copy(
                    top,
                    buf.at[(levels + 1,) + inner],
                    level_send.at[step, 0],
                    level_recv.at[step, 0],
                    (grp, tile - 1),
                    MESH,
                ),
            ),
            (
                tile < tiles - 1,
                tile > 0,
                pltpu.make_async_remote_copy(
                    bottom,
                    buf.at[(0,) + inner],
                    level_send.at[step, 1],
                    level_recv.at[step, 1],
                    (grp, tile + 1),
                    MESH,
                ),
            ),
        ]

    def row_copies(buf, step, slot, first, count):
        span = pl.ds(first + 1, count)
        across = pl.ds(LANE, columns)
        top, bottom = state_ref.at[:, pl.ds(0, 1), :], state_ref.at[:, pl.ds(rows - 1, 1), :]
        if step:
            top = buf.at[span, pl.ds(SUB, 1), across]
            bottom = buf.at[span, pl.ds(SUB + rows - 1, 1), across]
        return [
            (
                grp > 0,
                grp < grps - 1,
                pltpu.make_async_remote_copy(
                    top,
                    buf.at[span, pl.ds(SUB + rows, 1), across],
                    row_send.at[slot, 0],
                    row_recv.at[slot, 0],
                    (grp - 1, tile),
                    MESH,
                ),
            ),
            (
                grp < grps - 1,
                grp > 0,
                pltpu.make_async_remote_copy(
                    bottom,
                    buf.at[span, pl.ds(SUB - 1, 1), across],
                    row_send.at[slot, 1],
                    row_recv.at[slot, 1],
                    (grp + 1, tile),
                    MESH,
                ),
            ),
        ]

    def start(copies):
        for sends, _, copy in copies:
            pl.when(sends)(copy.start)

    def arrive(copies):
        for _, receives, copy in copies:
            pl.when(receives)(copy.wait_recv)

    def leave(copies):
        for sends, _, copy in copies:
            pl.when(sends)(copy.wait_send)

    def advance(src, dst, pad, first, count, row_first, row_count, at, width, edge=0, slot=0):
        if count <= 0 or row_count <= 0:
            return
        pieces = [(k, min(WIDTH, width - k)) for k in range(0, width, WIDTH)]

        @pl.loop(0, count * row_count, unroll=2)
        def _(i):
            level = first + lax.div(i, row_count)
            row = pl.multiple_of((row_first + lax.rem(i, row_count)) * SUB, SUB)
            rr = pl.ds(row, SUB)
            middle = pl.ds(row + SUB, SUB)
            for k, wide_by in pieces:
                here = pl.ds(pl.multiple_of(at + k, LANE), wide_by)
                mid = pl.ds(pl.multiple_of(at + k + LANE, LANE), wide_by)
                around = wide_by + 2 * LANE
                wide = src[level + 1, middle, pl.ds(pl.multiple_of(at + k, LANE), around)]
                center = wide[:, LANE : LANE + wide_by]
                e = pltpu.roll(wide, around - 1, 1)[:, LANE : LANE + wide_by]
                w = pltpu.roll(wide, 1, 1)[:, LANE : LANE + wide_by]
                index = lax.broadcasted_iota(jnp.int32, (SUB, wide_by), 0)
                n, s = center, center
                if edge <= 0:
                    down = src[level + 1, pl.ds(row + 2 * SUB, SUB), mid]
                    n = jnp.where(index == 0, down, center)
                if edge >= 0:
                    up = src[level + 1, pl.ds(row, SUB), mid]
                    s = jnp.where(index == SUB - 1, up, center)
                n = pltpu.roll(n, SUB - 1, 0)
                s = pltpu.roll(s, 1, 0)
                a = src[level, middle, mid]
                b = src[level + 2, middle, mid]
                flow = east[level, rr, here] * (e - w) + north[level, rr, here] * (n - s)
                value = (
                    (0.3 * center + misfit[level, rr, here])
                    + 0.5 * flow
                    + (0.1 * ((e + w) + (n + s)) + 0.15 * (a + b))
                )
                value = land[level, rr, here].astype(jnp.float32) * value
                if pad:
                    dst[level + 1, middle, mid] = value
                else:
                    dst[level - first + slot, rr, here] = value

    def forward(first, count, chunk_list, far, same, since, begin=0, end=pairs):
        if count <= 0:
            return
        base = (1 - side if far else side) * half
        base = base + (parity if same else 1 - parity)
        mine_at = pl.ds(tile * levels + first, count)

        def send(r, other, start, width):
            source = s2.at[pl.ds(first, count), pl.ds(r * SUB, SUB), pl.ds(start, width)]
            target = pencil.at[mine_at, pl.ds(r * SUB, SUB), :]
            if r == uneven:
                target = pencil_u.at[mine_at, :, pl.ds(0, width)]
            if other is None:
                pltpu.make_async_copy(source, target, fwd_recv.at[r]).start()
            else:
                pltpu.make_async_remote_copy(
                    source, target, fwd_send, fwd_recv.at[r], (grp, other), MESH
                ).start()

        local = not far and same
        for r in chunk_list:

            @pl.loop(max(begin, 1) if local else begin, end)
            def _(i):
                other = base + 2 * lax.rem(since + i, pairs)
                if r == uneven:
                    by_width(other, lambda width: send(r, other, uneven_start(other), width))
                else:
                    send(r, other, pl.multiple_of(other * part, LANE), part)

            if local:
                if r == uneven:
                    by_width(tile, lambda width: send(r, None, uneven_start(tile), width))
                else:
                    send(r, None, pl.multiple_of(tile * part, LANE), part)

    inner_chunks = list(range(1, chunks - 1))
    outer_chunks = [0, chunks - 1]
    all_chunks = inner_chunks + outer_chunks
    level0 = level_copies(s0, 0)
    row0 = row_copies(s0, 0, 0, 0, levels)

    def enter():
        pl.semaphore_wait(barrier, tiles - 1 + beside)
        start(level0)
        start(row0)

    def first_step(at, width):
        advance(s0, s1, True, 1, inside, 0, 1, at, width, edge=-1)
        advance(s0, s1, True, 1, inside, 1, chunks - 2, at, width)
        advance(s0, s1, True, 1, inside, chunks - 1, 1, at, width, edge=1)

    for copy in loads[0]:
        copy.wait()
    enter()
    first_step(*lead_wide)
    advance(s1, s2, False, near, early, 1, chunks - 2, *lead)
    forward(0, early, inner_chunks, True, True, head, 0, 1)

    for copy in loads[1]:
        copy.wait()
    first_step(*rest_wide)
    advance(s1, s2, False, near, early, 1, chunks - 2, *rest)
    forward(0, early, inner_chunks, True, True, head, 1, pairs)

    for copy in loads[2]:
        copy.wait()
    advance(s0, s1, True, 1, inside, 1, chunks - 2, *home_wide)
    arrive(row0)
    advance(s0, s1, True, 1, inside, 0, 1, *every)
    advance(s0, s1, True, 1, inside, chunks - 1, 1, *every)
    level1 = level_copies(s1, 1)
    row_mid = row_copies(s1, 1, 1, 1, levels - 2) if levels > 2 else []
    row_ends = row_copies(s1, 1, 2, 0, 1) + row_copies(s1, 1, 3, levels - 1, 1)
    start(row_mid)
    advance(s1, s2, False, near, early, 1, chunks - 2, *home)
    arrive(row_mid)
    for r in outer_chunks:
        advance(s1, s2, False, near, early, r, 1, *every)

    @pl.when(light)
    def _():
        forward(0, early, outer_chunks, True, True, turn)

    arrive(level0)
    advance(s0, s1, True, 0, 1, 0, chunks, *every)
    advance(s0, s1, True, levels - 1, 1, 0, chunks, *every)
    start(level1)
    start(row_ends)
    forward(0, early, inner_chunks, True, False, turn)

    @pl.when(light)
    def _():
        forward(0, early, outer_chunks, True, False, turn)


    advance(s1, s2, False, 1, near - 1, 0, chunks, *every, slot=early)
    advance(s1, s2, False, levels - near, near - 1, 0, chunks, *every, slot=early + near - 1)
    forward(early, 2 * near - 2, inner_chunks, True, True, turn)
    forward(early, 2 * near - 2, inner_chunks, True, False, turn)

    @pl.when(light)
    def _():
        forward(early, 2 * near - 2, outer_chunks, True, True, turn)
        forward(early, 2 * near - 2, outer_chunks, True, False, turn)

    forward(0, early, all_chunks, False, True, turn)
    forward(early, 2 * near - 2, all_chunks, False, True, turn)

    total = tiles * levels
    size = total * SUB
    row_of = lax.shift_right_logical(lax.broadcasted_iota(jnp.int32, (size, total), 0), 3)
    level_of = lax.broadcasted_iota(jnp.int32, (size, total), 1)
    repeat = (row_of == level_of).astype(jnp.float32)
    in_tile = lax.rem(row_of, levels)
    natural = jnp.where(
        in_tile < early,
        in_tile + near,
        jnp.where(
            in_tile < levels - 2,
            1 + (in_tile - early) * (levels - 3),
            (in_tile - (levels - 2)) * (levels - 1),
        ),
    )
    pick = (row_of - in_tile + natural == level_of).astype(jnp.float32)
    tall = jnp.dot(repeat, matrix[...], precision=HIGHEST, preferred_element_type=jnp.float32)
    full = lax.dot_general(
        tall,
        pick,
        (((1,), (1,)), ((), ())),
        precision=HIGHEST,
        preferred_element_type=jnp.float32,
    )
    same_row = (lax.broadcasted_iota(jnp.int32, (size, size), 0) & (SUB - 1)) == (
        lax.broadcasted_iota(jnp.int32, (size, size), 1) & (SUB - 1)
    )
    kron[...] = jnp.where(same_row, full, 0.0)

    arrive(level1)
    arrive(row_ends)
    for r in all_chunks:
        advance(s1, s2, False, 0, 1, r, 1, *every, slot=levels - 2)
        advance(s1, s2, False, levels - 1, 1, r, 1, *every, slot=levels - 1)
        for same in (True, False):
            if r in inner_chunks:
                forward(levels - 2, 2, [r], True, same, turn)
            else:
                pl.when(light)(lambda: forward(levels - 2, 2, [r], True, same, turn))
                pl.when(jnp.logical_not(light))(lambda: forward(0, levels, [r], True, same, turn))
        forward(levels - 2, 2, [r], False, True, turn)
        forward(0, levels, [r], False, False, turn)

    def give(source, place):
        def to(other):
            pltpu.make_async_remote_copy(
                source(other), place, ret_send, ret_recv, (grp, other), MESH
            ).start()

        @pl.loop(0, half)
        def _(i):
            to((1 - side) * half + i)

        @pl.loop(1, half)
        def _(i):
            to(side * half + lax.rem(lax.rem(tile, half) + i, half))

        pltpu.make_async_copy(source(tile), place, ret_recv).start()

    def smoothed(block, width):
        return jnp.dot(
            kron[...],
            block.reshape(size, width),
            precision=HIGHEST,
            preferred_element_type=jnp.float32,
        )

    def finish(r):
        span = pl.ds(r * SUB, SUB)
        chunk = pencil.at[:, span, :]
        pltpu.make_async_copy(chunk, chunk, fwd_recv.at[r]).wait()
        result = smoothed(pencil[:, r * SUB : (r + 1) * SUB, :], part)
        smooth[:, r * SUB : (r + 1) * SUB, :] = result.reshape(tiles * levels, SUB, part)
        give(
            lambda other: smooth.at[pl.ds(other * levels, levels), span, :],
            out_ref.at[:, span, pl.ds(pl.multiple_of(tile * part, LANE), part)],
        )
        surface_ref[r * SUB : (r + 1) * SUB, :] = (
            select[r * SUB : (r + 1) * SUB, :].astype(jnp.float32) * result[0:SUB]
        )

    strip = pltpu.make_async_remote_copy(
        smooth_u.at[0, :, pl.ds(pl.multiple_of((1 - side) * part, LANE), LANE)],
        border,
        border_sem.at[0],
        border_sem.at[1],
        (grp, partner),
        MESH,
    )

    def finish_uneven(width):
        span = pl.ds(uneven * SUB, SUB)
        across = pl.ds(0, width)
        chunk = pencil_u.at[:, :, across]
        pltpu.make_async_copy(chunk, chunk, fwd_recv.at[uneven]).wait()
        result = smoothed(pencil_u[:, :, 0:width], width)
        smooth_u[:, :, 0:width] = result.reshape(tiles * levels, SUB, width)
        give(
            lambda other: smooth_u.at[pl.ds(other * levels, levels), :, across],
            out_ref.at[:, span, pl.ds(uneven_start(tile), width)],
        )
        if width > part:
            strip.start()
            own = smooth_u[0, :, pl.ds(pl.multiple_of(side * LANE, LANE), part)]
            surface_ref[span, :] = select[span, :].astype(jnp.float32) * own
        else:
            at = pl.ds(pl.multiple_of((1 - side) * LANE, LANE), width)
            surface_ref[span, at] = select[span, at].astype(jnp.float32) * smooth_u[0, :, across]

    for r in all_chunks:
        if r == uneven:
            by_width(tile, finish_uneven)
        else:
            finish(r)

    def settle(width):
        span = pl.ds(uneven * SUB, SUB)
        if width > part:
            strip.wait_send()
        else:
            strip.wait_recv()
            at = pl.ds(pl.multiple_of(side * width, LANE), LANE)
            surface_ref[span, at] = select[span, at].astype(jnp.float32) * border[...]
        sent = s2.at[:, span, pl.ds(0, columns - width)]
        pltpu.make_async_copy(sent, sent, fwd_send).wait()
        returned = smooth_u.at[pl.ds(0, (tiles - 1) * levels), :, pl.ds(0, width)]
        pltpu.make_async_copy(returned, returned, ret_send).wait()

    by_width(tile, settle)
    for copies in (level0, row0, level1, row_mid, row_ends):
        leave(copies)
    even_rows = pl.ds(0, rows - SUB)
    sent = s2.at[:, even_rows, pl.ds(0, (tiles - 1) * part)]
    pltpu.make_async_copy(sent, sent, fwd_send).wait()
    returned = smooth.at[pl.ds(0, (tiles - 1) * levels), even_rows]
    pltpu.make_async_copy(returned, returned, ret_send).wait()
    pltpu.make_async_copy(out_ref, out_ref, ret_recv).wait()


def store(out_ref, surface_ref, out_hbm, surface_hbm, sem):
    copies = [
        pltpu.make_async_copy(out_ref, out_hbm, sem.at[0]),
        pltpu.make_async_copy(surface_ref, surface_hbm, sem.at[1]),
    ]
    for copy in copies:
        copy.start()
    for copy in copies:
        copy.wait()


def body(tiles, grps, *args):
    levels, rows, columns = args[0].shape
    part = columns // tiles
    total = tiles * levels
    padded = (levels + 2, rows + 2 * SUB, columns + 2 * LANE)
    block = (levels, rows, columns)
    hbm = pl.BlockSpec(memory_space=pltpu.HBM)
    vmem = pl.BlockSpec(memory_space=pltpu.VMEM)
    held = pl.pallas_call(
        functools.partial(kernel, tiles, grps),
        out_shape=(
            pltpu.VMEM(block, jnp.float32),
            pltpu.VMEM((rows, part), jnp.float32),
        ),
        in_specs=[hbm] * 7,
        out_specs=(vmem, vmem),
        scratch_shapes=[
            pltpu.VMEM(padded, jnp.float32),
            pltpu.VMEM(padded, jnp.float32),
            pltpu.VMEM(block, jnp.float32),
            pltpu.VMEM(block, jnp.float32),
            pltpu.VMEM(block, jnp.float32),
            pltpu.VMEM(block, jnp.float32),
            pltpu.VMEM(block, jnp.int32),
            pltpu.VMEM((total, rows, part), jnp.float32),
            pltpu.VMEM((total, rows, part), jnp.float32),
            pltpu.VMEM((total * SUB, total * SUB), jnp.float32),
            pltpu.VMEM((total, total), jnp.float32),
            pltpu.VMEM((rows, part), jnp.int32),
            pltpu.VMEM((total, SUB, part + LANE), jnp.float32),
            pltpu.VMEM((total, SUB, part + LANE), jnp.float32),
            pltpu.VMEM((SUB, LANE), jnp.float32),
            pltpu.SemaphoreType.DMA((25,)),
            pltpu.SemaphoreType.DMA((2, 2)),
            pltpu.SemaphoreType.DMA((2, 2)),
            pltpu.SemaphoreType.DMA((4, 2)),
            pltpu.SemaphoreType.DMA((4, 2)),
            pltpu.SemaphoreType.DMA,
            pltpu.SemaphoreType.DMA((rows // SUB,)),
            pltpu.SemaphoreType.DMA,
            pltpu.SemaphoreType.DMA,
            pltpu.SemaphoreType.DMA((2,)),
        ],
        compiler_params=pltpu.CompilerParams(
            collective_id=0, has_side_effects=True, vmem_limit_bytes=40 * 1024 * 1024
        ),
    )(*[pltpu.with_memory_space_constraint(arg, pltpu.HBM) for arg in args])
    return pl.pallas_call(
        store,
        out_shape=(
            jax.ShapeDtypeStruct(block, jnp.float32),
            jax.ShapeDtypeStruct((rows, part), jnp.float32),
        ),
        in_specs=[vmem] * 2,
        out_specs=(hbm, hbm),
        scratch_shapes=[pltpu.SemaphoreType.DMA((2,))],
        compiler_params=pltpu.CompilerParams(vmem_limit_bytes=1024 * 1024),
    )(*held)


def solution(mesh):
    split = P("tile", "grp", None)
    return jax.shard_map(
        functools.partial(body, mesh.shape["tile"], mesh.shape["grp"]),
        mesh=mesh,
        in_specs=(split,) * 5 + (P("grp", "tile"), P()),
        out_specs=(split, P("grp", "tile")),
        check_vma=False,
    )
```

```python
import functools

import jax
import jax.numpy as jnp
from jax import lax
from jax.experimental import pallas as pl
from jax.experimental.pallas import tpu as pltpu
from jax.sharding import PartitionSpec as P

MESH = pl.DeviceIdType.MESH
SUB = 8
LANE = 128
WIDTH = 512
HIGHEST = lax.Precision.HIGHEST


def kernel(
    tiles,
    grps,
    state_ref,
    misfit_ref,
    east_ref,
    north_ref,
    land_ref,
    select_ref,
    matrix_ref,
    out_ref,
    surface_ref,
    s0,
    s1,
    s2,
    misfit,
    east,
    north,
    land,
    pencil,
    smooth,
    kron,
    matrix,
    select,
    pencil_u,
    smooth_u,
    border,
    load_sem,
    level_send,
    level_recv,
    row_send,
    row_recv,
    fwd_send,
    fwd_recv,
    ret_send,
    ret_recv,
    border_sem,
):
    levels, rows, columns = state_ref.shape
    chunks = rows // SUB
    part = columns // tiles
    half = tiles // 2
    mine = columns // 2
    near = min(2, levels // 2)
    tile = lax.axis_index("tile")
    grp = lax.axis_index("grp")
    side = lax.div(tile, half)
    uneven = 0
    widths = (part + LANE, part - LANE)
    wide_here = lax.rem(tile, 2) == side
    partner = tile + 1 - 2 * lax.rem(tile, 2)

    def uneven_start(other):
        odd = lax.rem(other, 2)
        shift = odd * (1 - 2 * lax.div(other, half)) * LANE
        return pl.multiple_of(other * part + shift, LANE)

    def by_width(other, run):
        wide = lax.rem(other, 2) == lax.div(other, half)
        pl.when(wide)(lambda: run(widths[0]))
        pl.when(jnp.logical_not(wide))(lambda: run(widths[1]))
    inner = (pl.ds(SUB, rows), pl.ds(LANE, columns))

    early = levels - 2 * near
    inside = levels - 2
    pair = 2 * part
    pairs = half // 2
    parity = lax.rem(tile, 2)
    light = parity == side
    turn = lax.div(lax.rem(tile, half), 2)

    head = side * (pairs - 1)
    lead = (pl.multiple_of(mine - side * pair, LANE), pair)
    rest = (pl.multiple_of((1 - side) * (mine + pair), LANE), mine - pair)
    home = (pl.multiple_of(side * mine, LANE), mine)
    lead_wide = (pl.multiple_of(mine - side * pair - LANE, LANE), pair + 2 * LANE)
    rest_wide = (pl.multiple_of((1 - side) * (mine + pair + LANE), LANE), mine - pair - LANE)
    home_wide = (pl.multiple_of(side * (mine + LANE), LANE), mine - LANE)
    every = (0, columns)

    def state_load(at, width, k):
        return pltpu.make_async_copy(
            state_ref.at[:, :, pl.ds(at, width)],
            s0.at[pl.ds(1, levels), pl.ds(SUB, rows), pl.ds(at + LANE, width)],
            load_sem.at[k],
        )

    def field_loads(at, first, count, k):
        span = (pl.ds(first, count), slice(None), pl.ds(*at))
        return [
            pltpu.make_async_copy(ref.at[span], buf.at[span], load_sem.at[k + n])
            for n, (ref, buf) in enumerate(fields)
        ]

    fields = ((misfit_ref, misfit), (east_ref, east), (north_ref, north), (land_ref, land))
    loads = [
        [state_load(pl.multiple_of(mine - side * pair - 2 * LANE, LANE), pair + 4 * LANE, 0)],
        [
            state_load(pl.multiple_of(side * (mine + 2 * LANE), LANE), mine - 2 * LANE, 1),
            state_load(
                pl.multiple_of((1 - side) * (mine + pair + 2 * LANE), LANE),
                mine - pair - 2 * LANE,
                2,
            ),
        ]
        + field_loads(rest_wide, 0, levels, 3),
        field_loads(home_wide, 0, levels, 7)
        + field_loads(lead_wide, 0, 1, 11)
        + field_loads(lead_wide, levels - 1, 1, 15),
    ]
    if inside > 0:
        loads[0] += field_loads(lead_wide, 1, inside, 19)
    loads[2] += [
        pltpu.make_async_copy(matrix_ref, matrix, load_sem.at[23]),
        pltpu.make_async_copy(select_ref, select, load_sem.at[24]),
    ]

    barrier = pltpu.get_barrier_semaphore()

    @pl.loop(1, tiles)
    def _(i):
        other = lax.rem(tile + i, tiles)
        pl.semaphore_signal(barrier, inc=1, device_id=(grp, other), device_id_type=MESH)

    @pl.when(grp > 0)
    def _():
        pl.semaphore_signal(barrier, inc=1, device_id=(grp - 1, tile), device_id_type=MESH)

    @pl.when(grp < grps - 1)
    def _():
        pl.semaphore_signal(barrier, inc=1, device_id=(grp + 1, tile), device_id_type=MESH)

    for copy in loads[0] + loads[1] + loads[2]:
        copy.start()

    for buf in (s0, s1):
        for start in (0, columns + LANE):
            buf[1 : levels + 1, SUB : SUB + rows, start : start + LANE] = jnp.zeros(
                (levels, rows, LANE), jnp.float32
            )

        @pl.when(tile == 0)
        def _():
            buf[0, SUB : SUB + rows, :] = jnp.zeros((rows, columns + 2 * LANE), jnp.float32)

        @pl.when(tile == tiles - 1)
        def _():
            buf[levels + 1, SUB : SUB + rows, :] = jnp.zeros((rows, columns + 2 * LANE), jnp.float32)

        @pl.when(grp == 0)
        def _():
            buf[1 : levels + 1, 0:SUB, :] = jnp.zeros((levels, SUB, columns + 2 * LANE), jnp.float32)

        @pl.when(grp == grps - 1)
        def _():
            buf[1 : levels + 1, SUB + rows :, :] = jnp.zeros(
                (levels, SUB, columns + 2 * LANE), jnp.float32
            )

    beside = (grp > 0).astype(jnp.int32) + (grp < grps - 1).astype(jnp.int32)

    def level_copies(buf, step):
        top, bottom = state_ref.at[0], state_ref.at[levels - 1]
        if step:
            top, bottom = buf.at[(1,) + inner], buf.at[(levels,) + inner]
        return [
            (
                tile > 0,
                tile < tiles - 1,
                pltpu.make_async_remote_copy(
                    top,
                    buf.at[(levels + 1,) + inner],
                    level_send.at[step, 0],
                    level_recv.at[step, 0],
                    (grp, tile - 1),
                    MESH,
                ),
            ),
            (
                tile < tiles - 1,
                tile > 0,
                pltpu.make_async_remote_copy(
                    bottom,
                    buf.at[(0,) + inner],
                    level_send.at[step, 1],
                    level_recv.at[step, 1],
                    (grp, tile + 1),
                    MESH,
                ),
            ),
        ]

    def row_copies(buf, step, slot, first, count):
        span = pl.ds(first + 1, count)
        across = pl.ds(LANE, columns)
        top, bottom = state_ref.at[:, pl.ds(0, 1), :], state_ref.at[:, pl.ds(rows - 1, 1), :]
        if step:
            top = buf.at[span, pl.ds(SUB, 1), across]
            bottom = buf.at[span, pl.ds(SUB + rows - 1, 1), across]
        return [
            (
                grp > 0,
                grp < grps - 1,
                pltpu.make_async_remote_copy(
                    top,
                    buf.at[span, pl.ds(SUB + rows, 1), across],
                    row_send.at[slot, 0],
                    row_recv.at[slot, 0],
                    (grp - 1, tile),
                    MESH,
                ),
            ),
            (
                grp < grps - 1,
                grp > 0,
                pltpu.make_async_remote_copy(
                    bottom,
                    buf.at[span, pl.ds(SUB - 1, 1), across],
                    row_send.at[slot, 1],
                    row_recv.at[slot, 1],
                    (grp + 1, tile),
                    MESH,
                ),
            ),
        ]

    def start(copies):
        for sends, _, copy in copies:
            pl.when(sends)(copy.start)

    def arrive(copies):
        for _, receives, copy in copies:
            pl.when(receives)(copy.wait_recv)

    def leave(copies):
        for sends, _, copy in copies:
            pl.when(sends)(copy.wait_send)

    def advance(src, dst, pad, first, count, row_first, row_count, at, width, edge=0, slot=0):
        if count <= 0 or row_count <= 0:
            return
        pieces = [(k, min(WIDTH, width - k)) for k in range(0, width, WIDTH)]

        @pl.loop(0, count * row_count, unroll=2)
        def _(i):
            level = first + lax.div(i, row_count)
            row = pl.multiple_of((row_first + lax.rem(i, row_count)) * SUB, SUB)
            rr = pl.ds(row, SUB)
            middle = pl.ds(row + SUB, SUB)
            for k, wide_by in pieces:
                here = pl.ds(pl.multiple_of(at + k, LANE), wide_by)
                mid = pl.ds(pl.multiple_of(at + k + LANE, LANE), wide_by)
                around = wide_by + 2 * LANE
                wide = src[level + 1, middle, pl.ds(pl.multiple_of(at + k, LANE), around)]
                center = wide[:, LANE : LANE + wide_by]
                e = pltpu.roll(wide, around - 1, 1)[:, LANE : LANE + wide_by]
                w = pltpu.roll(wide, 1, 1)[:, LANE : LANE + wide_by]
                index = lax.broadcasted_iota(jnp.int32, (SUB, wide_by), 0)
                n, s = center, center
                if edge <= 0:
                    down = src[level + 1, pl.ds(row + 2 * SUB, SUB), mid]
                    n = jnp.where(index == 0, down, center)
                if edge >= 0:
                    up = src[level + 1, pl.ds(row, SUB), mid]
                    s = jnp.where(index == SUB - 1, up, center)
                n = pltpu.roll(n, SUB - 1, 0)
                s = pltpu.roll(s, 1, 0)
                a = src[level, middle, mid]
                b = src[level + 2, middle, mid]
                flow = east[level, rr, here] * (e - w) + north[level, rr, here] * (n - s)
                value = (
                    (0.3 * center + misfit[level, rr, here])
                    + 0.5 * flow
                    + (0.1 * ((e + w) + (n + s)) + 0.15 * (a + b))
                )
                value = land[level, rr, here].astype(jnp.float32) * value
                if pad:
                    dst[level + 1, middle, mid] = value
                else:
                    dst[level - first + slot, rr, here] = value

    def forward(first, count, chunk_list, far, same, since, begin=0, end=pairs):
        if count <= 0:
            return
        base = (1 - side if far else side) * half
        base = base + (parity if same else 1 - parity)
        mine_at = pl.ds(tile * levels + first, count)

        def send(r, other, start, width):
            source = s2.at[pl.ds(first, count), pl.ds(r * SUB, SUB), pl.ds(start, width)]
            target = pencil.at[mine_at, pl.ds(r * SUB, SUB), :]
            if r == uneven:
                target = pencil_u.at[mine_at, :, pl.ds(0, width)]
            if other is None:
                pltpu.make_async_copy(source, target, fwd_recv.at[r]).start()
            else:
                pltpu.make_async_remote_copy(
                    source, target, fwd_send, fwd_recv.at[r], (grp, other), MESH
                ).start()

        local = not far and same
        for r in chunk_list:

            @pl.loop(max(begin, 1) if local else begin, end)
            def _(i):
                other = base + 2 * lax.rem(since + i, pairs)
                if r == uneven:
                    by_width(other, lambda width: send(r, other, uneven_start(other), width))
                else:
                    send(r, other, pl.multiple_of(other * part, LANE), part)

            if local:
                if r == uneven:
                    by_width(tile, lambda width: send(r, None, uneven_start(tile), width))
                else:
                    send(r, None, pl.multiple_of(tile * part, LANE), part)

    inner_chunks = list(range(1, chunks - 1))
    outer_chunks = [0, chunks - 1]
    all_chunks = inner_chunks + outer_chunks
    level0 = level_copies(s0, 0)
    row0 = row_copies(s0, 0, 0, 0, levels)

    def enter():
        pl.semaphore_wait(barrier, tiles - 1 + beside)
        start(level0)
        start(row0)

    def first_step(at, width):
        advance(s0, s1, True, 1, inside, 0, 1, at, width, edge=-1)
        advance(s0, s1, True, 1, inside, 1, chunks - 2, at, width)
        advance(s0, s1, True, 1, inside, chunks - 1, 1, at, width, edge=1)

    for copy in loads[0]:
        copy.wait()
    enter()
    first_step(*lead_wide)
    advance(s1, s2, False, near, early, 1, chunks - 2, *lead)
    forward(0, early, inner_chunks, True, True, head, 0, 1)

    for copy in loads[1]:
        copy.wait()
    first_step(*rest_wide)
    advance(s1, s2, False, near, early, 1, chunks - 2, *rest)
    forward(0, early, inner_chunks, True, True, head, 1, pairs)

    for copy in loads[2]:
        copy.wait()
    advance(s0, s1, True, 1, inside, 1, chunks - 2, *home_wide)
    arrive(row0)
    advance(s0, s1, True, 1, inside, 0, 1, *every)
    advance(s0, s1, True, 1, inside, chunks - 1, 1, *every)
    level1 = level_copies(s1, 1)
    row_mid = row_copies(s1, 1, 1, 1, levels - 2) if levels > 2 else []
    row_ends = row_copies(s1, 1, 2, 0, 1) + row_copies(s1, 1, 3, levels - 1, 1)
    start(row_mid)
    advance(s1, s2, False, near, early, 1, chunks - 2, *home)
    arrive(row_mid)
    for r in outer_chunks:
        advance(s1, s2, False, near, early, r, 1, *every)

    @pl.when(light)
    def _():
        forward(0, early, outer_chunks, True, True, turn)

    arrive(level0)
    advance(s0, s1, True, 0, 1, 0, chunks, *every)
    advance(s0, s1, True, levels - 1, 1, 0, chunks, *every)
    start(level1)
    start(row_ends)
    forward(0, early, inner_chunks, True, False, turn)

    @pl.when(light)
    def _():
        forward(0, early, outer_chunks, True, False, turn)


    advance(s1, s2, False, 1, near - 1, 0, chunks, *every, slot=early)
    advance(s1, s2, False, levels - near, near - 1, 0, chunks, *every, slot=early + near - 1)
    forward(early, 2 * near - 2, inner_chunks, True, True, turn)
    forward(early, 2 * near - 2, inner_chunks, True, False, turn)

    @pl.when(light)
    def _():
        forward(early, 2 * near - 2, outer_chunks, True, True, turn)
        forward(early, 2 * near - 2, outer_chunks, True, False, turn)


    total = tiles * levels
    size = total * SUB
    row_of = lax.shift_right_logical(lax.broadcasted_iota(jnp.int32, (size, total), 0), 3)
    level_of = lax.broadcasted_iota(jnp.int32, (size, total), 1)
    repeat = (row_of == level_of).astype(jnp.float32)
    in_tile = lax.rem(row_of, levels)
    natural = jnp.where(
        in_tile < early,
        in_tile + near,
        jnp.where(
            in_tile < levels - 2,
            1 + (in_tile - early) * (levels - 3),
            (in_tile - (levels - 2)) * (levels - 1),
        ),
    )
    pick = (row_of - in_tile + natural == level_of).astype(jnp.float32)
    tall = jnp.dot(repeat, matrix[...], precision=HIGHEST, preferred_element_type=jnp.float32)
    full = lax.dot_general(
        tall,
        pick,
        (((1,), (1,)), ((), ())),
        precision=HIGHEST,
        preferred_element_type=jnp.float32,
    )
    same_row = (lax.broadcasted_iota(jnp.int32, (size, size), 0) & (SUB - 1)) == (
        lax.broadcasted_iota(jnp.int32, (size, size), 1) & (SUB - 1)
    )
    kron[...] = jnp.where(same_row, full, 0.0)

    arrive(level1)
    arrive(row_ends)
    for r in all_chunks:
        advance(s1, s2, False, 0, 1, r, 1, *every, slot=levels - 2)
        advance(s1, s2, False, levels - 1, 1, r, 1, *every, slot=levels - 1)
        for same in (True, False):
            if r in inner_chunks:
                forward(levels - 2, 2, [r], True, same, turn)
            else:
                pl.when(light)(lambda: forward(levels - 2, 2, [r], True, same, turn))
                pl.when(jnp.logical_not(light))(lambda: forward(0, levels, [r], True, same, turn))
        forward(0, levels, [r], False, True, turn)
        forward(0, levels, [r], False, False, turn)

    def give(source, place):
        def to(other):
            pltpu.make_async_remote_copy(
                source(other), place, ret_send, ret_recv, (grp, other), MESH
            ).start()

        @pl.loop(0, half)
        def _(i):
            to((1 - side) * half + i)

        @pl.loop(1, half)
        def _(i):
            to(side * half + lax.rem(lax.rem(tile, half) + i, half))

        pltpu.make_async_copy(source(tile), place, ret_recv).start()

    def smoothed(block, width):
        return jnp.dot(
            kron[...],
            block.reshape(size, width),
            precision=HIGHEST,
            preferred_element_type=jnp.float32,
        )

    def finish(r):
        span = pl.ds(r * SUB, SUB)
        chunk = pencil.at[:, span, :]
        pltpu.make_async_copy(chunk, chunk, fwd_recv.at[r]).wait()
        result = smoothed(pencil[:, r * SUB : (r + 1) * SUB, :], part)
        smooth[:, r * SUB : (r + 1) * SUB, :] = result.reshape(tiles * levels, SUB, part)
        give(
            lambda other: smooth.at[pl.ds(other * levels, levels), span, :],
            out_ref.at[:, span, pl.ds(pl.multiple_of(tile * part, LANE), part)],
        )
        surface_ref[r * SUB : (r + 1) * SUB, :] = (
            select[r * SUB : (r + 1) * SUB, :].astype(jnp.float32) * result[0:SUB]
        )

    strip = pltpu.make_async_remote_copy(
        smooth_u.at[0, :, pl.ds(pl.multiple_of((1 - side) * part, LANE), LANE)],
        border,
        border_sem.at[0],
        border_sem.at[1],
        (grp, partner),
        MESH,
    )

    def finish_uneven(width):
        span = pl.ds(uneven * SUB, SUB)
        across = pl.ds(0, width)
        chunk = pencil_u.at[:, :, across]
        pltpu.make_async_copy(chunk, chunk, fwd_recv.at[uneven]).wait()
        result = smoothed(pencil_u[:, :, 0:width], width)
        smooth_u[:, :, 0:width] = result.reshape(tiles * levels, SUB, width)
        give(
            lambda other: smooth_u.at[pl.ds(other * levels, levels), :, across],
            out_ref.at[:, span, pl.ds(uneven_start(tile), width)],
        )
        if width > part:
            strip.start()
            own = smooth_u[0, :, pl.ds(pl.multiple_of(side * LANE, LANE), part)]
            surface_ref[span, :] = select[span, :].astype(jnp.float32) * own
        else:
            at = pl.ds(pl.multiple_of((1 - side) * LANE, LANE), width)
            surface_ref[span, at] = select[span, at].astype(jnp.float32) * smooth_u[0, :, across]

    for r in all_chunks:
        if r == uneven:
            by_width(tile, finish_uneven)
        else:
            finish(r)

    def settle(width):
        span = pl.ds(uneven * SUB, SUB)
        if width > part:
            strip.wait_send()
        else:
            strip.wait_recv()
            at = pl.ds(pl.multiple_of(side * width, LANE), LANE)
            surface_ref[span, at] = select[span, at].astype(jnp.float32) * border[...]
        sent = s2.at[:, span, pl.ds(0, columns - width)]
        pltpu.make_async_copy(sent, sent, fwd_send).wait()
        returned = smooth_u.at[pl.ds(0, (tiles - 1) * levels), :, pl.ds(0, width)]
        pltpu.make_async_copy(returned, returned, ret_send).wait()

    by_width(tile, settle)
    for copies in (level0, row0, level1, row_mid, row_ends):
        leave(copies)
    even_rows = pl.ds(0, rows - SUB)
    sent = s2.at[:, even_rows, pl.ds(0, (tiles - 1) * part)]
    pltpu.make_async_copy(sent, sent, fwd_send).wait()
    returned = smooth.at[pl.ds(0, (tiles - 1) * levels), even_rows]
    pltpu.make_async_copy(returned, returned, ret_send).wait()
    pltpu.make_async_copy(out_ref, out_ref, ret_recv).wait()


def store(out_ref, surface_ref, out_hbm, surface_hbm, sem):
    copies = [
        pltpu.make_async_copy(out_ref, out_hbm, sem.at[0]),
        pltpu.make_async_copy(surface_ref, surface_hbm, sem.at[1]),
    ]
    for copy in copies:
        copy.start()
    for copy in copies:
        copy.wait()


def body(tiles, grps, *args):
    levels, rows, columns = args[0].shape
    part = columns // tiles
    total = tiles * levels
    padded = (levels + 2, rows + 2 * SUB, columns + 2 * LANE)
    block = (levels, rows, columns)
    hbm = pl.BlockSpec(memory_space=pltpu.HBM)
    vmem = pl.BlockSpec(memory_space=pltpu.VMEM)
    held = pl.pallas_call(
        functools.partial(kernel, tiles, grps),
        out_shape=(
            pltpu.VMEM(block, jnp.float32),
            pltpu.VMEM((rows, part), jnp.float32),
        ),
        in_specs=[hbm] * 7,
        out_specs=(vmem, vmem),
        scratch_shapes=[
            pltpu.VMEM(padded, jnp.float32),
            pltpu.VMEM(padded, jnp.float32),
            pltpu.VMEM(block, jnp.float32),
            pltpu.VMEM(block, jnp.float32),
            pltpu.VMEM(block, jnp.float32),
            pltpu.VMEM(block, jnp.float32),
            pltpu.VMEM(block, jnp.int32),
            pltpu.VMEM((total, rows, part), jnp.float32),
            pltpu.VMEM((total, rows, part), jnp.float32),
            pltpu.VMEM((total * SUB, total * SUB), jnp.float32),
            pltpu.VMEM((total, total), jnp.float32),
            pltpu.VMEM((rows, part), jnp.int32),
            pltpu.VMEM((total, SUB, part + LANE), jnp.float32),
            pltpu.VMEM((total, SUB, part + LANE), jnp.float32),
            pltpu.VMEM((SUB, LANE), jnp.float32),
            pltpu.SemaphoreType.DMA((25,)),
            pltpu.SemaphoreType.DMA((2, 2)),
            pltpu.SemaphoreType.DMA((2, 2)),
            pltpu.SemaphoreType.DMA((4, 2)),
            pltpu.SemaphoreType.DMA((4, 2)),
            pltpu.SemaphoreType.DMA,
            pltpu.SemaphoreType.DMA((rows // SUB,)),
            pltpu.SemaphoreType.DMA,
            pltpu.SemaphoreType.DMA,
            pltpu.SemaphoreType.DMA((2,)),
        ],
        compiler_params=pltpu.CompilerParams(
            collective_id=0, has_side_effects=True, vmem_limit_bytes=40 * 1024 * 1024
        ),
    )(*[pltpu.with_memory_space_constraint(arg, pltpu.HBM) for arg in args])
    return pl.pallas_call(
        store,
        out_shape=(
            jax.ShapeDtypeStruct(block, jnp.float32),
            jax.ShapeDtypeStruct((rows, part), jnp.float32),
        ),
        in_specs=[vmem] * 2,
        out_specs=(hbm, hbm),
        scratch_shapes=[pltpu.SemaphoreType.DMA((2,))],
        compiler_params=pltpu.CompilerParams(vmem_limit_bytes=1024 * 1024, skip_device_barrier=True),
    )(*held)


def solution(mesh):
    split = P("tile", "grp", None)
    return jax.shard_map(
        functools.partial(body, mesh.shape["tile"], mesh.shape["grp"]),
        mesh=mesh,
        in_specs=(split,) * 5 + (P("grp", "tile"), P()),
        out_specs=(split, P("grp", "tile")),
        check_vma=False,
    )
```

```python
import functools

import jax
import jax.numpy as jnp
from jax import lax
from jax.experimental import pallas as pl
from jax.experimental.pallas import tpu as pltpu
from jax.sharding import PartitionSpec as P

MESH = pl.DeviceIdType.MESH
SUB = 8
LANE = 128
WIDTH = 512
HIGHEST = lax.Precision.HIGHEST


def kernel(
    tiles,
    grps,
    state_ref,
    misfit_ref,
    east_ref,
    north_ref,
    land_ref,
    select_ref,
    matrix_ref,
    out_ref,
    surface_ref,
    s0,
    s1,
    s2,
    misfit,
    east,
    north,
    land,
    pencil,
    smooth,
    kron,
    matrix,
    select,
    pencil_u,
    smooth_u,
    border,
    load_sem,
    level_send,
    level_recv,
    row_send,
    row_recv,
    fwd_send,
    fwd_recv,
    ret_send,
    ret_recv,
    border_sem,
    joined,
):
    levels, rows, columns = state_ref.shape
    chunks = rows // SUB
    part = columns // tiles
    half = tiles // 2
    mine = columns // 2
    near = min(2, levels // 2)
    tile = lax.axis_index("tile")
    grp = lax.axis_index("grp")
    side = lax.div(tile, half)
    uneven = 0
    widths = (part + LANE, part - LANE)
    wide_here = lax.rem(tile, 2) == side
    partner = tile + 1 - 2 * lax.rem(tile, 2)

    def uneven_start(other):
        odd = lax.rem(other, 2)
        shift = odd * (1 - 2 * lax.div(other, half)) * LANE
        return pl.multiple_of(other * part + shift, LANE)

    def by_width(other, run):
        wide = lax.rem(other, 2) == lax.div(other, half)
        pl.when(wide)(lambda: run(widths[0]))
        pl.when(jnp.logical_not(wide))(lambda: run(widths[1]))
    inner = (pl.ds(SUB, rows), pl.ds(LANE, columns))

    early = levels - 2 * near
    inside = levels - 2
    pair = 2 * part
    pairs = half // 2
    parity = lax.rem(tile, 2)
    light = parity == side
    flip = parity
    turn = lax.div(lax.rem(tile, half), 2)

    head = side * (pairs - 1)
    lead = (pl.multiple_of(mine - side * pair, LANE), pair)
    rest = (pl.multiple_of((1 - side) * (mine + pair), LANE), mine - pair)
    home = (pl.multiple_of(side * mine, LANE), mine)
    lead_wide = (pl.multiple_of(mine - side * pair - LANE, LANE), pair + 2 * LANE)
    rest_wide = (pl.multiple_of((1 - side) * (mine + pair + LANE), LANE), mine - pair - LANE)
    home_wide = (pl.multiple_of(side * (mine + LANE), LANE), mine - LANE)
    every = (0, columns)

    def state_load(at, width, k):
        return pltpu.make_async_copy(
            state_ref.at[:, :, pl.ds(at, width)],
            s0.at[pl.ds(1, levels), pl.ds(SUB, rows), pl.ds(at + LANE, width)],
            load_sem.at[k],
        )

    def field_loads(at, first, count, k):
        span = (pl.ds(first, count), slice(None), pl.ds(*at))
        return [
            pltpu.make_async_copy(ref.at[span], buf.at[span], load_sem.at[k + n])
            for n, (ref, buf) in enumerate(fields)
        ]

    fields = ((misfit_ref, misfit), (east_ref, east), (north_ref, north), (land_ref, land))
    loads = [
        [state_load(pl.multiple_of(mine - side * pair - 2 * LANE, LANE), pair + 4 * LANE, 0)],
        [
            state_load(pl.multiple_of(side * (mine + 2 * LANE), LANE), mine - 2 * LANE, 1),
            state_load(
                pl.multiple_of((1 - side) * (mine + pair + 2 * LANE), LANE),
                mine - pair - 2 * LANE,
                2,
            ),
        ]
        + field_loads(rest_wide, 0, levels, 3),
        field_loads(home_wide, 0, levels, 7)
        + field_loads(lead_wide, 0, 1, 11)
        + field_loads(lead_wide, levels - 1, 1, 15),
    ]
    if inside > 0:
        loads[0] += field_loads(lead_wide, 1, inside, 19)
    loads[2] += [
        pltpu.make_async_copy(matrix_ref, matrix, load_sem.at[23]),
        pltpu.make_async_copy(select_ref, select, load_sem.at[24]),
    ]

    barrier = pltpu.get_barrier_semaphore()

    late = tile >= tiles - 2

    @pl.when(jnp.logical_not(late))
    def _():
        @pl.loop(1, tiles)
        def _(i):
            other = lax.rem(tile + i, tiles)
            pl.semaphore_signal(barrier, inc=1, device_id=(grp, other), device_id_type=MESH)

    @pl.when(late)
    def _():
        pl.semaphore_signal(barrier, inc=1, device_id=(grp, partner), device_id_type=MESH)

    @pl.when(grp > 0)
    def _():
        pl.semaphore_signal(barrier, inc=1, device_id=(grp - 1, tile), device_id_type=MESH)

    @pl.when(grp < grps - 1)
    def _():
        pl.semaphore_signal(barrier, inc=1, device_id=(grp + 1, tile), device_id_type=MESH)

    for copy in loads[0] + loads[1] + loads[2]:
        copy.start()

    for buf in (s0, s1):
        for start in (0, columns + LANE):
            buf[1 : levels + 1, SUB : SUB + rows, start : start + LANE] = jnp.zeros(
                (levels, rows, LANE), jnp.float32
            )

        @pl.when(tile == 0)
        def _():
            buf[0, SUB : SUB + rows, :] = jnp.zeros((rows, columns + 2 * LANE), jnp.float32)

        @pl.when(tile == tiles - 1)
        def _():
            buf[levels + 1, SUB : SUB + rows, :] = jnp.zeros((rows, columns + 2 * LANE), jnp.float32)

        @pl.when(grp == 0)
        def _():
            buf[1 : levels + 1, 0:SUB, :] = jnp.zeros((levels, SUB, columns + 2 * LANE), jnp.float32)

        @pl.when(grp == grps - 1)
        def _():
            buf[1 : levels + 1, SUB + rows :, :] = jnp.zeros(
                (levels, SUB, columns + 2 * LANE), jnp.float32
            )

    beside = (grp > 0).astype(jnp.int32) + (grp < grps - 1).astype(jnp.int32)

    def level_copies(buf, step):
        top, bottom = state_ref.at[0], state_ref.at[levels - 1]
        if step:
            top, bottom = buf.at[(1,) + inner], buf.at[(levels,) + inner]
        return [
            (
                tile > 0,
                tile < tiles - 1,
                pltpu.make_async_remote_copy(
                    top,
                    buf.at[(levels + 1,) + inner],
                    level_send.at[step, 0],
                    level_recv.at[step, 0],
                    (grp, tile - 1),
                    MESH,
                ),
            ),
            (
                tile < tiles - 1,
                tile > 0,
                pltpu.make_async_remote_copy(
                    bottom,
                    buf.at[(0,) + inner],
                    level_send.at[step, 1],
                    level_recv.at[step, 1],
                    (grp, tile + 1),
                    MESH,
                ),
            ),
        ]

    def row_copies(buf, step, slot, first, count):
        span = pl.ds(first + 1, count)
        across = pl.ds(LANE, columns)
        top, bottom = state_ref.at[:, pl.ds(0, 1), :], state_ref.at[:, pl.ds(rows - 1, 1), :]
        if step:
            top = buf.at[span, pl.ds(SUB, 1), across]
            bottom = buf.at[span, pl.ds(SUB + rows - 1, 1), across]
        return [
            (
                grp > 0,
                grp < grps - 1,
                pltpu.make_async_remote_copy(
                    top,
                    buf.at[span, pl.ds(SUB + rows, 1), across],
                    row_send.at[slot, 0],
                    row_recv.at[slot, 0],
                    (grp - 1, tile),
                    MESH,
                ),
            ),
            (
                grp < grps - 1,
                grp > 0,
                pltpu.make_async_remote_copy(
                    bottom,
                    buf.at[span, pl.ds(SUB - 1, 1), across],
                    row_send.at[slot, 1],
                    row_recv.at[slot, 1],
                    (grp + 1, tile),
                    MESH,
                ),
            ),
        ]

    def start(copies):
        for sends, _, copy in copies:
            pl.when(sends)(copy.start)

    def arrive(copies):
        for _, receives, copy in copies:
            pl.when(receives)(copy.wait_recv)

    def leave(copies):
        for sends, _, copy in copies:
            pl.when(sends)(copy.wait_send)

    def advance(src, dst, pad, first, count, row_first, row_count, at, width, edge=0, slot=0, unroll=2):
        if count <= 0 or row_count <= 0:
            return
        pieces = [(k, min(WIDTH, width - k)) for k in range(0, width, WIDTH)]

        @pl.loop(0, count * row_count, unroll=unroll)
        def _(i):
            level = first + lax.div(i, row_count)
            row = pl.multiple_of((row_first + lax.rem(i, row_count)) * SUB, SUB)
            rr = pl.ds(row, SUB)
            middle = pl.ds(row + SUB, SUB)
            for k, wide_by in pieces:
                here = pl.ds(pl.multiple_of(at + k, LANE), wide_by)
                mid = pl.ds(pl.multiple_of(at + k + LANE, LANE), wide_by)
                around = wide_by + 2 * LANE
                wide = src[level + 1, middle, pl.ds(pl.multiple_of(at + k, LANE), around)]
                center = wide[:, LANE : LANE + wide_by]
                e = pltpu.roll(wide, around - 1, 1)[:, LANE : LANE + wide_by]
                w = pltpu.roll(wide, 1, 1)[:, LANE : LANE + wide_by]
                index = lax.broadcasted_iota(jnp.int32, (SUB, wide_by), 0)
                n, s = center, center
                if edge <= 0:
                    down = src[level + 1, pl.ds(row + 2 * SUB, SUB), mid]
                    n = jnp.where(index == 0, down, center)
                if edge >= 0:
                    up = src[level + 1, pl.ds(row, SUB), mid]
                    s = jnp.where(index == SUB - 1, up, center)
                n = pltpu.roll(n, SUB - 1, 0)
                s = pltpu.roll(s, 1, 0)
                a = src[level, middle, mid]
                b = src[level + 2, middle, mid]
                flow = east[level, rr, here] * (e - w) + north[level, rr, here] * (n - s)
                value = (
                    (0.3 * center + misfit[level, rr, here])
                    + 0.5 * flow
                    + (0.1 * ((e + w) + (n + s)) + 0.15 * (a + b))
                )
                value = land[level, rr, here].astype(jnp.float32) * value
                if pad:
                    dst[level + 1, middle, mid] = value
                else:
                    dst[level - first + slot, rr, here] = value

    def forward(first, count, chunk_list, far, same, since, begin=0, end=pairs):
        if count <= 0:
            return
        base = (1 - side if far else side) * half
        base = base + (parity if same else 1 - parity)
        mine_at = pl.ds(tile * levels + first, count)

        def send(r, other, start, width):
            source = s2.at[pl.ds(first, count), pl.ds(r * SUB, SUB), pl.ds(start, width)]
            target = pencil.at[mine_at, pl.ds(r * SUB, SUB), :]
            if r == uneven:
                target = pencil_u.at[mine_at, :, pl.ds(0, width)]
            if other is None:
                pltpu.make_async_copy(source, target, fwd_recv.at[r]).start()
            else:
                pltpu.make_async_remote_copy(
                    source, target, fwd_send, fwd_recv.at[r], (grp, other), MESH
                ).start()

        local = not far and same
        for r in chunk_list:

            @pl.loop(max(begin, 1) if local else begin, end)
            def _(i):
                other = base + 2 * lax.rem(since + i, pairs)
                if r == uneven:
                    by_width(other, lambda width: send(r, other, uneven_start(other), width))
                else:
                    send(r, other, pl.multiple_of(other * part, LANE), part)

            if local:
                if r == uneven:
                    by_width(tile, lambda width: send(r, None, uneven_start(tile), width))
                else:
                    send(r, None, pl.multiple_of(tile * part, LANE), part)

    inner_chunks = list(range(1, chunks - 1))
    outer_chunks = [0, chunks - 1]
    all_chunks = inner_chunks + outer_chunks
    level0 = level_copies(s0, 0)
    row0 = row_copies(s0, 0, 0, 0, levels)

    def enter():
        pl.semaphore_wait(barrier, jnp.where(late, tiles - 1, tiles - 3) + beside)

        @pl.when(late)
        def _():
            @pl.loop(0, tiles - 2)
            def _(other):
                pl.semaphore_signal(joined, inc=1, device_id=(grp, other), device_id_type=MESH)

        sends, _, up = level0[1]
        start([level0[0], (sends & (tile != tiles - 3), None, up)])
        start(row0)

    def first_step(at, width):
        advance(s0, s1, True, 1, inside, 0, 1, at, width, edge=-1)
        advance(s0, s1, True, 1, inside, 1, chunks - 2, at, width)
        advance(s0, s1, True, 1, inside, chunks - 1, 1, at, width, edge=1)

    enter()
    for copy in loads[0]:
        copy.wait()

    @pl.when(tile == tiles - 3)
    def _():
        pl.semaphore_wait(joined, 2)
        level0[1][2].start()

    advance(s0, s1, True, 1, inside, 0, 1, *lead_wide, edge=-1, unroll=3)
    advance(s0, s1, True, 1, inside, 1, chunks - 2, *lead_wide, unroll=3)
    advance(s1, s2, False, near, early, 1, chunks - 3, *lead)
    forward(0, early, inner_chunks[:-1], True, True, head, 0, 1)
    advance(s0, s1, True, 1, inside, chunks - 1, 1, *lead_wide, edge=1, unroll=3)
    advance(s1, s2, False, near, early, chunks - 2, 1, *lead)
    forward(0, early, inner_chunks[-1:], True, True, head, 0, 1)

    @pl.when(tile < tiles - 3)
    def _():
        pl.semaphore_wait(joined, 2)

    for copy in loads[1]:
        copy.wait()
    first_step(*rest_wide)
    advance(s1, s2, False, near, early, 1, chunks - 2, *rest)
    forward(0, early, inner_chunks, True, True, head, 1, pairs)

    for copy in loads[2]:
        copy.wait()
    advance(s0, s1, True, 1, inside, 1, chunks - 2, *home_wide)
    arrive(row0)
    advance(s0, s1, True, 1, inside, 0, 1, *every)
    advance(s0, s1, True, 1, inside, chunks - 1, 1, *every)
    level1 = level_copies(s1, 1)
    row_mid = row_copies(s1, 1, 1, 1, levels - 2) if levels > 2 else []
    row_ends = row_copies(s1, 1, 2, 0, 1) + row_copies(s1, 1, 3, levels - 1, 1)
    start(row_mid)
    advance(s1, s2, False, near, early, 1, chunks - 2, *home)
    arrive(row_mid)
    for r in outer_chunks:
        advance(s1, s2, False, near, early, r, 1, *every)

    @pl.when(light)
    def _():
        forward(0, early, outer_chunks, True, True, turn)

    arrive(level0)
    advance(s0, s1, True, 0, 1, 0, chunks, *every)
    advance(s0, s1, True, levels - 1, 1, 0, chunks, *every)
    start(level1)
    start(row_ends)
    forward(0, early, inner_chunks, True, False, turn)

    @pl.when(light)
    def _():
        forward(0, early, outer_chunks, True, False, turn)


    advance(s1, s2, False, 1, near - 1, 0, chunks, *every, slot=early)
    advance(s1, s2, False, levels - near, near - 1, 0, chunks, *every, slot=early + near - 1)
    forward(early, 2 * near - 2, inner_chunks, True, True, turn)
    forward(early, 2 * near - 2, inner_chunks, True, False, turn)

    @pl.when(light)
    def _():
        forward(early, 2 * near - 2, outer_chunks, True, True, turn)
        forward(early, 2 * near - 2, outer_chunks, True, False, turn)

    forward(0, early, all_chunks, False, True, turn)
    forward(early, 2 * near - 2, all_chunks, False, True, turn)

    total = tiles * levels
    size = total * SUB
    row_of = lax.shift_right_logical(lax.broadcasted_iota(jnp.int32, (size, total), 0), 3)
    level_of = lax.broadcasted_iota(jnp.int32, (size, total), 1)
    repeat = (row_of == level_of).astype(jnp.float32)
    in_tile = lax.rem(row_of, levels)
    natural = jnp.where(
        in_tile < early,
        in_tile + near,
        jnp.where(
            in_tile < levels - 2,
            1 + (in_tile - early) * (levels - 3),
            (in_tile - (levels - 2)) * (levels - 1),
        ),
    )
    pick = (row_of - in_tile + natural == level_of).astype(jnp.float32)
    tall = jnp.dot(repeat, matrix[...], precision=HIGHEST, preferred_element_type=jnp.float32)
    full = lax.dot_general(
        tall,
        pick,
        (((1,), (1,)), ((), ())),
        precision=HIGHEST,
        preferred_element_type=jnp.float32,
    )
    same_row = (lax.broadcasted_iota(jnp.int32, (size, size), 0) & (SUB - 1)) == (
        lax.broadcasted_iota(jnp.int32, (size, size), 1) & (SUB - 1)
    )
    kron[...] = jnp.where(same_row, full, 0.0)

    arrive(level1)
    arrive(row_ends)
    for r in all_chunks:
        advance(s1, s2, False, 0, 1, r, 1, *every, slot=levels - 2)
        advance(s1, s2, False, levels - 1, 1, r, 1, *every, slot=levels - 1)
        for same in (True, False):
            if r in inner_chunks:
                forward(levels - 2, 2, [r], True, same, turn)
            else:
                pl.when(light)(lambda: forward(levels - 2, 2, [r], True, same, turn))
                pl.when(jnp.logical_not(light))(lambda: forward(0, levels, [r], True, same, turn))
        forward(levels - 2, 2, [r], False, True, turn)
        forward(0, levels, [r], False, False, turn)

    def give(source, place):
        def to(other):
            pltpu.make_async_remote_copy(
                source(other), place, ret_send, ret_recv, (grp, other), MESH
            ).start()

        @pl.loop(0, half)
        def _(i):
            to((1 - side) * half + i - lax.rem(i, 2) + lax.rem(i + flip, 2))

        @pl.loop(1, half)
        def _(i):
            to(side * half + lax.rem(lax.rem(tile, half) + i, half))

        pltpu.make_async_copy(source(tile), place, ret_recv).start()

    def smoothed(block, width):
        return jnp.dot(
            kron[...],
            block.reshape(size, width),
            precision=HIGHEST,
            preferred_element_type=jnp.float32,
        )

    def finish(r):
        span = pl.ds(r * SUB, SUB)
        chunk = pencil.at[:, span, :]
        pltpu.make_async_copy(chunk, chunk, fwd_recv.at[r]).wait()
        result = smoothed(pencil[:, r * SUB : (r + 1) * SUB, :], part)
        smooth[:, r * SUB : (r + 1) * SUB, :] = result.reshape(tiles * levels, SUB, part)
        give(
            lambda other: smooth.at[pl.ds(other * levels, levels), span, :],
            out_ref.at[:, span, pl.ds(pl.multiple_of(tile * part, LANE), part)],
        )
        surface_ref[r * SUB : (r + 1) * SUB, :] = (
            select[r * SUB : (r + 1) * SUB, :].astype(jnp.float32) * result[0:SUB]
        )

    strip = pltpu.make_async_remote_copy(
        smooth_u.at[0, :, pl.ds(pl.multiple_of((1 - side) * part, LANE), LANE)],
        border,
        border_sem.at[0],
        border_sem.at[1],
        (grp, partner),
        MESH,
    )

    def finish_uneven(width):
        span = pl.ds(uneven * SUB, SUB)
        across = pl.ds(0, width)
        chunk = pencil_u.at[:, :, across]
        pltpu.make_async_copy(chunk, chunk, fwd_recv.at[uneven]).wait()
        result = smoothed(pencil_u[:, :, 0:width], width)
        smooth_u[:, :, 0:width] = result.reshape(tiles * levels, SUB, width)
        give(
            lambda other: smooth_u.at[pl.ds(other * levels, levels), :, across],
            out_ref.at[:, span, pl.ds(uneven_start(tile), width)],
        )
        if width > part:
            strip.start()
            own = smooth_u[0, :, pl.ds(pl.multiple_of(side * LANE, LANE), part)]
            surface_ref[span, :] = select[span, :].astype(jnp.float32) * own
        else:
            at = pl.ds(pl.multiple_of((1 - side) * LANE, LANE), width)
            surface_ref[span, at] = select[span, at].astype(jnp.float32) * smooth_u[0, :, across]

    for r in all_chunks:
        if r == uneven:
            by_width(tile, finish_uneven)
        else:
            finish(r)

    def settle(width):
        span = pl.ds(uneven * SUB, SUB)
        if width > part:
            strip.wait_send()
        else:
            strip.wait_recv()
            at = pl.ds(pl.multiple_of(side * width, LANE), LANE)
            surface_ref[span, at] = select[span, at].astype(jnp.float32) * border[...]
        sent = s2.at[:, span, pl.ds(0, columns - width)]
        pltpu.make_async_copy(sent, sent, fwd_send).wait()
        returned = smooth_u.at[pl.ds(0, (tiles - 1) * levels), :, pl.ds(0, width)]
        pltpu.make_async_copy(returned, returned, ret_send).wait()

    by_width(tile, settle)
    for copies in (level0, row0, level1, row_mid, row_ends):
        leave(copies)
    even_rows = pl.ds(0, rows - SUB)
    sent = s2.at[:, even_rows, pl.ds(0, (tiles - 1) * part)]
    pltpu.make_async_copy(sent, sent, fwd_send).wait()
    returned = smooth.at[pl.ds(0, (tiles - 1) * levels), even_rows]
    pltpu.make_async_copy(returned, returned, ret_send).wait()
    pltpu.make_async_copy(out_ref, out_ref, ret_recv).wait()


def store(out_ref, surface_ref, out_hbm, surface_hbm, sem):
    copies = [
        pltpu.make_async_copy(out_ref, out_hbm, sem.at[0]),
        pltpu.make_async_copy(surface_ref, surface_hbm, sem.at[1]),
    ]
    for copy in copies:
        copy.start()
    for copy in copies:
        copy.wait()


def body(tiles, grps, *args):
    levels, rows, columns = args[0].shape
    part = columns // tiles
    total = tiles * levels
    padded = (levels + 2, rows + 2 * SUB, columns + 2 * LANE)
    block = (levels, rows, columns)
    hbm = pl.BlockSpec(memory_space=pltpu.HBM)
    vmem = pl.BlockSpec(memory_space=pltpu.VMEM)
    held = pl.pallas_call(
        functools.partial(kernel, tiles, grps),
        out_shape=(
            pltpu.VMEM(block, jnp.float32),
            pltpu.VMEM((rows, part), jnp.float32),
        ),
        in_specs=[hbm] * 7,
        out_specs=(vmem, vmem),
        scratch_shapes=[
            pltpu.VMEM(padded, jnp.float32),
            pltpu.VMEM(padded, jnp.float32),
            pltpu.VMEM(block, jnp.float32),
            pltpu.VMEM(block, jnp.float32),
            pltpu.VMEM(block, jnp.float32),
            pltpu.VMEM(block, jnp.float32),
            pltpu.VMEM(block, jnp.int32),
            pltpu.VMEM((total, rows, part), jnp.float32),
            pltpu.VMEM((total, rows, part), jnp.float32),
            pltpu.VMEM((total * SUB, total * SUB), jnp.float32),
            pltpu.VMEM((total, total), jnp.float32),
            pltpu.VMEM((rows, part), jnp.int32),
            pltpu.VMEM((total, SUB, part + LANE), jnp.float32),
            pltpu.VMEM((total, SUB, part + LANE), jnp.float32),
            pltpu.VMEM((SUB, LANE), jnp.float32),
            pltpu.SemaphoreType.DMA((25,)),
            pltpu.SemaphoreType.DMA((2, 2)),
            pltpu.SemaphoreType.DMA((2, 2)),
            pltpu.SemaphoreType.DMA((4, 2)),
            pltpu.SemaphoreType.DMA((4, 2)),
            pltpu.SemaphoreType.DMA,
            pltpu.SemaphoreType.DMA((rows // SUB,)),
            pltpu.SemaphoreType.DMA,
            pltpu.SemaphoreType.DMA,
            pltpu.SemaphoreType.DMA((2,)),
            pltpu.SemaphoreType.REGULAR,
        ],
        compiler_params=pltpu.CompilerParams(
            collective_id=0, has_side_effects=True, vmem_limit_bytes=40 * 1024 * 1024
        ),
    )(*[pltpu.with_memory_space_constraint(arg, pltpu.HBM) for arg in args])
    return pl.pallas_call(
        store,
        out_shape=(
            jax.ShapeDtypeStruct(block, jnp.float32),
            jax.ShapeDtypeStruct((rows, part), jnp.float32),
        ),
        in_specs=[vmem] * 2,
        out_specs=(hbm, hbm),
        scratch_shapes=[pltpu.SemaphoreType.DMA((2,))],
        compiler_params=pltpu.CompilerParams(vmem_limit_bytes=1024 * 1024),
    )(*held)


def solution(mesh):
    split = P("tile", "grp", None)
    return jax.shard_map(
        functools.partial(body, mesh.shape["tile"], mesh.shape["grp"]),
        mesh=mesh,
        in_specs=(split,) * 5 + (P("grp", "tile"), P()),
        out_specs=(split, P("grp", "tile")),
        check_vma=False,
    )
```

```python
import functools

import jax
import jax.numpy as jnp
from jax import lax
from jax.experimental import pallas as pl
from jax.experimental.pallas import tpu as pltpu
from jax.sharding import PartitionSpec as P

MESH = pl.DeviceIdType.MESH
SUB = 8
LANE = 128
WIDTH = 512
HIGHEST = lax.Precision.HIGHEST


def kernel(
    tiles,
    grps,
    state_ref,
    misfit_ref,
    east_ref,
    north_ref,
    land_ref,
    select_ref,
    matrix_ref,
    out_ref,
    surface_ref,
    s0,
    s1,
    s2,
    misfit,
    east,
    north,
    land,
    pencil,
    smooth,
    kron,
    matrix,
    select,
    pencil_u,
    smooth_u,
    border,
    load_sem,
    level_send,
    level_recv,
    row_send,
    row_recv,
    fwd_send,
    fwd_recv,
    ret_send,
    ret_recv,
    border_sem,
):
    levels, rows, columns = state_ref.shape
    chunks = rows // SUB
    part = columns // tiles
    half = tiles // 2
    mine = columns // 2
    near = min(2, levels // 2)
    tile = lax.axis_index("tile")
    grp = lax.axis_index("grp")
    side = lax.div(tile, half)
    uneven = 0
    widths = (part + LANE, part - LANE)
    wide_here = lax.rem(tile, 2) == side
    partner = tile + 1 - 2 * lax.rem(tile, 2)

    def uneven_start(other):
        odd = lax.rem(other, 2)
        shift = odd * (1 - 2 * lax.div(other, half)) * LANE
        return pl.multiple_of(other * part + shift, LANE)

    def by_width(other, run):
        wide = lax.rem(other, 2) == lax.div(other, half)
        pl.when(wide)(lambda: run(widths[0]))
        pl.when(jnp.logical_not(wide))(lambda: run(widths[1]))
    inner = (pl.ds(SUB, rows), pl.ds(LANE, columns))

    early = levels - 2 * near
    inside = levels - 2
    pair = 2 * part
    pairs = half // 2
    parity = lax.rem(tile, 2)
    light = parity == side
    turn = lax.div(lax.rem(tile, half), 2)

    head = side * (pairs - 1)
    lead = (pl.multiple_of(mine - side * pair, LANE), pair)
    rest = (pl.multiple_of((1 - side) * (mine + pair), LANE), mine - pair)
    home = (pl.multiple_of(side * mine, LANE), mine)
    lead_wide = (pl.multiple_of(mine - side * pair - LANE, LANE), pair + 2 * LANE)
    rest_wide = (pl.multiple_of((1 - side) * (mine + pair + LANE), LANE), mine - pair - LANE)
    home_wide = (pl.multiple_of(side * (mine + LANE), LANE), mine - LANE)
    every = (0, columns)

    def state_load(at, width, k):
        return pltpu.make_async_copy(
            state_ref.at[:, :, pl.ds(at, width)],
            s0.at[pl.ds(1, levels), pl.ds(SUB, rows), pl.ds(at + LANE, width)],
            load_sem.at[k],
        )

    def field_loads(at, first, count, k):
        span = (pl.ds(first, count), slice(None), pl.ds(*at))
        return [
            pltpu.make_async_copy(ref.at[span], buf.at[span], load_sem.at[k + n])
            for n, (ref, buf) in enumerate(fields)
        ]

    fields = ((misfit_ref, misfit), (east_ref, east), (north_ref, north), (land_ref, land))
    loads = [
        [state_load(pl.multiple_of(mine - side * pair - 2 * LANE, LANE), pair + 4 * LANE, 0)],
        [
            state_load(pl.multiple_of(side * (mine + 2 * LANE), LANE), mine - 2 * LANE, 1),
            state_load(
                pl.multiple_of((1 - side) * (mine + pair + 2 * LANE), LANE),
                mine - pair - 2 * LANE,
                2,
            ),
        ]
        + field_loads(rest_wide, 0, levels, 3),
        field_loads(home_wide, 0, levels, 7)
        + field_loads(lead_wide, 0, 1, 11)
        + field_loads(lead_wide, levels - 1, 1, 15),
    ]
    if inside > 0:
        loads[0] += field_loads(lead_wide, 1, inside, 19)
    loads[2] += [
        pltpu.make_async_copy(matrix_ref, matrix, load_sem.at[23]),
        pltpu.make_async_copy(select_ref, select, load_sem.at[24]),
    ]

    barrier = pltpu.get_barrier_semaphore()

    @pl.loop(1, tiles)
    def _(i):
        other = lax.rem(tile + i, tiles)
        pl.semaphore_signal(barrier, inc=1, device_id=(grp, other), device_id_type=MESH)

    @pl.when(grp > 0)
    def _():
        pl.semaphore_signal(barrier, inc=1, device_id=(grp - 1, tile), device_id_type=MESH)

    @pl.when(grp < grps - 1)
    def _():
        pl.semaphore_signal(barrier, inc=1, device_id=(grp + 1, tile), device_id_type=MESH)

    for copy in loads[0] + loads[1] + loads[2]:
        copy.start()

    for buf in (s0, s1):
        for start in (0, columns + LANE):
            buf[1 : levels + 1, SUB : SUB + rows, start : start + LANE] = jnp.zeros(
                (levels, rows, LANE), jnp.float32
            )

        @pl.when(tile == 0)
        def _():
            buf[0, SUB : SUB + rows, :] = jnp.zeros((rows, columns + 2 * LANE), jnp.float32)

        @pl.when(tile == tiles - 1)
        def _():
            buf[levels + 1, SUB : SUB + rows, :] = jnp.zeros((rows, columns + 2 * LANE), jnp.float32)

        @pl.when(grp == 0)
        def _():
            buf[1 : levels + 1, 0:SUB, :] = jnp.zeros((levels, SUB, columns + 2 * LANE), jnp.float32)

        @pl.when(grp == grps - 1)
        def _():
            buf[1 : levels + 1, SUB + rows :, :] = jnp.zeros(
                (levels, SUB, columns + 2 * LANE), jnp.float32
            )

    beside = (grp > 0).astype(jnp.int32) + (grp < grps - 1).astype(jnp.int32)

    def level_copies(buf, step):
        top, bottom = state_ref.at[0], state_ref.at[levels - 1]
        if step:
            top, bottom = buf.at[(1,) + inner], buf.at[(levels,) + inner]
        return [
            (
                tile > 0,
                tile < tiles - 1,
                pltpu.make_async_remote_copy(
                    top,
                    buf.at[(levels + 1,) + inner],
                    level_send.at[step, 0],
                    level_recv.at[step, 0],
                    (grp, tile - 1),
                    MESH,
                ),
            ),
            (
                tile < tiles - 1,
                tile > 0,
                pltpu.make_async_remote_copy(
                    bottom,
                    buf.at[(0,) + inner],
                    level_send.at[step, 1],
                    level_recv.at[step, 1],
                    (grp, tile + 1),
                    MESH,
                ),
            ),
        ]

    def row_copies(buf, step, slot, first, count):
        span = pl.ds(first + 1, count)
        across = pl.ds(LANE, columns)
        top, bottom = state_ref.at[:, pl.ds(0, 1), :], state_ref.at[:, pl.ds(rows - 1, 1), :]
        if step:
            top = buf.at[span, pl.ds(SUB, 1), across]
            bottom = buf.at[span, pl.ds(SUB + rows - 1, 1), across]
        return [
            (
                grp > 0,
                grp < grps - 1,
                pltpu.make_async_remote_copy(
                    top,
                    buf.at[span, pl.ds(SUB + rows, 1), across],
                    row_send.at[slot, 0],
                    row_recv.at[slot, 0],
                    (grp - 1, tile),
                    MESH,
                ),
            ),
            (
                grp < grps - 1,
                grp > 0,
                pltpu.make_async_remote_copy(
                    bottom,
                    buf.at[span, pl.ds(SUB - 1, 1), across],
                    row_send.at[slot, 1],
                    row_recv.at[slot, 1],
                    (grp + 1, tile),
                    MESH,
                ),
            ),
        ]

    def start(copies):
        for sends, _, copy in copies:
            pl.when(sends)(copy.start)

    def arrive(copies):
        for _, receives, copy in copies:
            pl.when(receives)(copy.wait_recv)

    def leave(copies):
        for sends, _, copy in copies:
            pl.when(sends)(copy.wait_send)

    def advance(src, dst, pad, first, count, row_first, row_count, at, width, edge=0, slot=0):
        if count <= 0 or row_count <= 0:
            return
        pieces = [(k, min(WIDTH, width - k)) for k in range(0, width, WIDTH)]

        @pl.loop(0, count * row_count, unroll=2)
        def _(i):
            level = first + lax.div(i, row_count)
            row = pl.multiple_of((row_first + lax.rem(i, row_count)) * SUB, SUB)
            rr = pl.ds(row, SUB)
            middle = pl.ds(row + SUB, SUB)
            for k, wide_by in pieces:
                here = pl.ds(pl.multiple_of(at + k, LANE), wide_by)
                mid = pl.ds(pl.multiple_of(at + k + LANE, LANE), wide_by)
                around = wide_by + 2 * LANE
                wide = src[level + 1, middle, pl.ds(pl.multiple_of(at + k, LANE), around)]
                center = wide[:, LANE : LANE + wide_by]
                e = pltpu.roll(wide, around - 1, 1)[:, LANE : LANE + wide_by]
                w = pltpu.roll(wide, 1, 1)[:, LANE : LANE + wide_by]
                index = lax.broadcasted_iota(jnp.int32, (SUB, wide_by), 0)
                n, s = center, center
                if edge <= 0:
                    down = src[level + 1, pl.ds(row + 2 * SUB, SUB), mid]
                    n = jnp.where(index == 0, down, center)
                if edge >= 0:
                    up = src[level + 1, pl.ds(row, SUB), mid]
                    s = jnp.where(index == SUB - 1, up, center)
                n = pltpu.roll(n, SUB - 1, 0)
                s = pltpu.roll(s, 1, 0)
                a = src[level, middle, mid]
                b = src[level + 2, middle, mid]
                flow = east[level, rr, here] * (e - w) + north[level, rr, here] * (n - s)
                value = (
                    (0.3 * center + misfit[level, rr, here])
                    + 0.5 * flow
                    + (0.1 * ((e + w) + (n + s)) + 0.15 * (a + b))
                )
                value = land[level, rr, here].astype(jnp.float32) * value
                if pad:
                    dst[level + 1, middle, mid] = value
                else:
                    dst[level - first + slot, rr, here] = value

    def forward(first, count, chunk_list, far, same, since, begin=0, end=pairs):
        if count <= 0:
            return
        base = (1 - side if far else side) * half
        base = base + (parity if same else 1 - parity)
        mine_at = pl.ds(tile * levels + first, count)

        def send(r, other, start, width):
            source = s2.at[pl.ds(first, count), pl.ds(r * SUB, SUB), pl.ds(start, width)]
            target = pencil.at[mine_at, pl.ds(r * SUB, SUB), :]
            if r == uneven:
                target = pencil_u.at[mine_at, :, pl.ds(0, width)]
            if other is None:
                pltpu.make_async_copy(source, target, fwd_recv.at[r]).start()
            else:
                pltpu.make_async_remote_copy(
                    source, target, fwd_send, fwd_recv.at[r], (grp, other), MESH
                ).start()

        local = not far and same
        for r in chunk_list:

            @pl.loop(max(begin, 1) if local else begin, end)
            def _(i):
                other = base + 2 * lax.rem(since + i, pairs)
                if r == uneven:
                    by_width(other, lambda width: send(r, other, uneven_start(other), width))
                else:
                    send(r, other, pl.multiple_of(other * part, LANE), part)

            if local:
                if r == uneven:
                    by_width(tile, lambda width: send(r, None, uneven_start(tile), width))
                else:
                    send(r, None, pl.multiple_of(tile * part, LANE), part)

    inner_chunks = list(range(1, chunks - 1))
    outer_chunks = [0, chunks - 1]
    all_chunks = inner_chunks + outer_chunks
    level0 = level_copies(s0, 0)
    row0 = row_copies(s0, 0, 0, 0, levels)

    def enter():
        pl.semaphore_wait(barrier, tiles - 1 + beside)
        start(level0)
        start(row0)

    def first_step(at, width):
        advance(s0, s1, True, 1, inside, 0, 1, at, width, edge=-1)
        advance(s0, s1, True, 1, inside, 1, chunks - 2, at, width)
        advance(s0, s1, True, 1, inside, chunks - 1, 1, at, width, edge=1)

    for copy in loads[0]:
        copy.wait()
    enter()
    first_step(*lead_wide)
    advance(s1, s2, False, near, early, 1, chunks - 2, *lead)
    forward(0, early, inner_chunks, True, True, head, 0, 1)

    for copy in loads[1]:
        copy.wait()
    first_step(*rest_wide)
    advance(s1, s2, False, near, early, 1, chunks - 2, *rest)
    forward(0, early, inner_chunks, True, True, head, 1, pairs)

    for copy in loads[2]:
        copy.wait()
    advance(s0, s1, True, 1, inside, 1, chunks - 2, *home_wide)
    arrive(row0)
    advance(s0, s1, True, 1, inside, 0, 1, *every)
    advance(s0, s1, True, 1, inside, chunks - 1, 1, *every)
    level1 = level_copies(s1, 1)
    row_mid = row_copies(s1, 1, 1, 1, levels - 2) if levels > 2 else []
    row_ends = row_copies(s1, 1, 2, 0, 1) + row_copies(s1, 1, 3, levels - 1, 1)
    start(row_mid)
    advance(s1, s2, False, near, early, 1, chunks - 2, *home)
    arrive(row_mid)
    for r in outer_chunks:
        advance(s1, s2, False, near, early, r, 1, *every)

    @pl.when(light)
    def _():
        forward(0, early, outer_chunks, True, True, turn)

    arrive(level0)
    advance(s0, s1, True, 0, 1, 0, chunks, *every)
    advance(s0, s1, True, levels - 1, 1, 0, chunks, *every)
    start(level1)
    start(row_ends)
    forward(0, early, inner_chunks, True, False, turn)

    @pl.when(light)
    def _():
        forward(0, early, outer_chunks, True, False, turn)


    advance(s1, s2, False, 1, near - 1, 0, chunks, *every, slot=early)
    advance(s1, s2, False, levels - near, near - 1, 0, chunks, *every, slot=early + near - 1)
    forward(early, 2 * near - 2, inner_chunks, True, True, turn)
    forward(early, 2 * near - 2, inner_chunks, True, False, turn)

    @pl.when(light)
    def _():
        forward(early, 2 * near - 2, outer_chunks, True, True, turn)
        forward(early, 2 * near - 2, outer_chunks, True, False, turn)

    forward(0, early, all_chunks, False, True, turn)
    forward(early, 2 * near - 2, all_chunks, False, True, turn)

    total = tiles * levels
    size = total * SUB
    row_of = lax.shift_right_logical(lax.broadcasted_iota(jnp.int32, (size, total), 0), 3)
    level_of = lax.broadcasted_iota(jnp.int32, (size, total), 1)
    repeat = (row_of == level_of).astype(jnp.float32)
    in_tile = lax.rem(row_of, levels)
    natural = jnp.where(
        in_tile < early,
        in_tile + near,
        jnp.where(
            in_tile < levels - 2,
            1 + (in_tile - early) * (levels - 3),
            (in_tile - (levels - 2)) * (levels - 1),
        ),
    )
    pick = (row_of - in_tile + natural == level_of).astype(jnp.float32)
    tall = jnp.dot(repeat, matrix[...], precision=HIGHEST, preferred_element_type=jnp.float32)
    full = lax.dot_general(
        tall,
        pick,
        (((1,), (1,)), ((), ())),
        precision=HIGHEST,
        preferred_element_type=jnp.float32,
    )
    same_row = (lax.broadcasted_iota(jnp.int32, (size, size), 0) & (SUB - 1)) == (
        lax.broadcasted_iota(jnp.int32, (size, size), 1) & (SUB - 1)
    )
    kron[...] = jnp.where(same_row, full, 0.0)

    arrive(level1)
    arrive(row_ends)
    for r in all_chunks:
        advance(s1, s2, False, 0, 1, r, 1, *every, slot=levels - 2)
        advance(s1, s2, False, levels - 1, 1, r, 1, *every, slot=levels - 1)
        for same in (True, False):
            if r in inner_chunks:
                forward(levels - 2, 2, [r], True, same, turn)
            else:
                pl.when(light)(lambda: forward(levels - 2, 2, [r], True, same, turn))
                pl.when(jnp.logical_not(light))(lambda: forward(0, levels, [r], True, same, turn))
        forward(levels - 2, 2, [r], False, True, turn)
        forward(0, levels, [r], False, False, turn)

    def give(source, place):
        def to(other):
            pltpu.make_async_remote_copy(
                source(other), place, ret_send, ret_recv, (grp, other), MESH
            ).start()

        @pl.loop(0, half)
        def _(i):
            to((1 - side) * half + i)

        @pl.loop(1, half)
        def _(i):
            to(side * half + lax.rem(lax.rem(tile, half) + i, half))

        pltpu.make_async_copy(source(tile), place, ret_recv).start()

    def smoothed(block, width):
        return jnp.dot(
            kron[...],
            block.reshape(size, width),
            precision=HIGHEST,
            preferred_element_type=jnp.float32,
        )

    def finish(r):
        span = pl.ds(r * SUB, SUB)
        chunk = pencil.at[:, span, :]
        pltpu.make_async_copy(chunk, chunk, fwd_recv.at[r]).wait()
        result = smoothed(pencil[:, r * SUB : (r + 1) * SUB, :], part)
        smooth[:, r * SUB : (r + 1) * SUB, :] = result.reshape(tiles * levels, SUB, part)
        give(
            lambda other: smooth.at[pl.ds(other * levels, levels), span, :],
            out_ref.at[:, span, pl.ds(pl.multiple_of(tile * part, LANE), part)],
        )
        surface_ref[r * SUB : (r + 1) * SUB, :] = (
            select[r * SUB : (r + 1) * SUB, :].astype(jnp.float32) * result[0:SUB]
        )

    strip = pltpu.make_async_remote_copy(
        smooth_u.at[0, :, pl.ds(pl.multiple_of((1 - side) * part, LANE), LANE)],
        border,
        border_sem.at[0],
        border_sem.at[1],
        (grp, partner),
        MESH,
    )

    def finish_uneven(width):
        span = pl.ds(uneven * SUB, SUB)
        across = pl.ds(0, width)
        chunk = pencil_u.at[:, :, across]
        pltpu.make_async_copy(chunk, chunk, fwd_recv.at[uneven]).wait()
        result = smoothed(pencil_u[:, :, 0:width], width)
        smooth_u[:, :, 0:width] = result.reshape(tiles * levels, SUB, width)
        give(
            lambda other: smooth_u.at[pl.ds(other * levels, levels), :, across],
            out_ref.at[:, span, pl.ds(uneven_start(tile), width)],
        )
        if width > part:
            strip.start()
            own = smooth_u[0, :, pl.ds(pl.multiple_of(side * LANE, LANE), part)]
            surface_ref[span, :] = select[span, :].astype(jnp.float32) * own
        else:
            at = pl.ds(pl.multiple_of((1 - side) * LANE, LANE), width)
            surface_ref[span, at] = select[span, at].astype(jnp.float32) * smooth_u[0, :, across]

    for r in all_chunks:
        if r == uneven:
            by_width(tile, finish_uneven)
        else:
            finish(r)

    def settle(width):
        span = pl.ds(uneven * SUB, SUB)
        if width > part:
            strip.wait_send()
        else:
            strip.wait_recv()
            at = pl.ds(pl.multiple_of(side * width, LANE), LANE)
            surface_ref[span, at] = select[span, at].astype(jnp.float32) * border[...]
        sent = s2.at[:, span, pl.ds(0, columns - width)]
        pltpu.make_async_copy(sent, sent, fwd_send).wait()
        returned = smooth_u.at[pl.ds(0, (tiles - 1) * levels), :, pl.ds(0, width)]
        pltpu.make_async_copy(returned, returned, ret_send).wait()

    by_width(tile, settle)
    for copies in (level0, row0, level1, row_mid, row_ends):
        leave(copies)
    even_rows = pl.ds(0, rows - SUB)
    sent = s2.at[:, even_rows, pl.ds(0, (tiles - 1) * part)]
    pltpu.make_async_copy(sent, sent, fwd_send).wait()
    returned = smooth.at[pl.ds(0, (tiles - 1) * levels), even_rows]
    pltpu.make_async_copy(returned, returned, ret_send).wait()
    pltpu.make_async_copy(out_ref, out_ref, ret_recv).wait()


def store(out_ref, surface_ref, out_hbm, surface_hbm, sem):
    copies = [
        pltpu.make_async_copy(out_ref, out_hbm, sem.at[0]),
        pltpu.make_async_copy(surface_ref, surface_hbm, sem.at[1]),
    ]
    for copy in copies:
        copy.start()
    for copy in copies:
        copy.wait()


def body(tiles, grps, *args):
    levels, rows, columns = args[0].shape
    part = columns // tiles
    total = tiles * levels
    padded = (levels + 2, rows + 2 * SUB, columns + 2 * LANE)
    block = (levels, rows, columns)
    hbm = pl.BlockSpec(memory_space=pltpu.HBM)
    vmem = pl.BlockSpec(memory_space=pltpu.VMEM)
    held = pl.pallas_call(
        functools.partial(kernel, tiles, grps),
        out_shape=(
            pltpu.VMEM(block, jnp.float32),
            pltpu.VMEM((rows, part), jnp.float32),
        ),
        in_specs=[hbm] * 7,
        out_specs=(vmem, vmem),
        scratch_shapes=[
            pltpu.VMEM(padded, jnp.float32),
            pltpu.VMEM(padded, jnp.float32),
            pltpu.VMEM(block, jnp.float32),
            pltpu.VMEM(block, jnp.float32),
            pltpu.VMEM(block, jnp.float32),
            pltpu.VMEM(block, jnp.float32),
            pltpu.VMEM(block, jnp.int32),
            pltpu.VMEM((total, rows, part), jnp.float32),
            pltpu.VMEM((total, rows, part), jnp.float32),
            pltpu.VMEM((total * SUB, total * SUB), jnp.float32),
            pltpu.VMEM((total, total), jnp.float32),
            pltpu.VMEM((rows, part), jnp.int32),
            pltpu.VMEM((total, SUB, part + LANE), jnp.float32),
            pltpu.VMEM((total, SUB, part + LANE), jnp.float32),
            pltpu.VMEM((SUB, LANE), jnp.float32),
            pltpu.SemaphoreType.DMA((25,)),
            pltpu.SemaphoreType.DMA((2, 2)),
            pltpu.SemaphoreType.DMA((2, 2)),
            pltpu.SemaphoreType.DMA((4, 2)),
            pltpu.SemaphoreType.DMA((4, 2)),
            pltpu.SemaphoreType.DMA,
            pltpu.SemaphoreType.DMA((rows // SUB,)),
            pltpu.SemaphoreType.DMA,
            pltpu.SemaphoreType.DMA,
            pltpu.SemaphoreType.DMA((2,)),
        ],
        compiler_params=pltpu.CompilerParams(
            collective_id=0, has_side_effects=True, vmem_limit_bytes=40 * 1024 * 1024
        ),
    )(*[pltpu.with_memory_space_constraint(arg, pltpu.HBM) for arg in args])
    return pl.pallas_call(
        store,
        out_shape=(
            jax.ShapeDtypeStruct(block, jnp.float32),
            jax.ShapeDtypeStruct((rows, part), jnp.float32),
        ),
        in_specs=[vmem] * 2,
        out_specs=(hbm, hbm),
        scratch_shapes=[pltpu.SemaphoreType.DMA((2,))],
        compiler_params=pltpu.CompilerParams(vmem_limit_bytes=1024 * 1024, skip_device_barrier=True),
    )(*held)


def solution(mesh):
    split = P("tile", "grp", None)
    return jax.shard_map(
        functools.partial(body, mesh.shape["tile"], mesh.shape["grp"]),
        mesh=mesh,
        in_specs=(split,) * 5 + (P("grp", "tile"), P()),
        out_specs=(split, P("grp", "tile")),
        check_vma=False,
    )
```
